32 devices in a mesh: space: 16 (over z, x, core), tm: 2 (over y).
Axes of the slice: x: 2, y: 2, z: 4, core: 2. Of those that a mesh axis runs over, the one named last changes fastest.
Arguments:
- start_state: float32 [2, 2, 256, 4096], P('tm', None, 'space'), may hold values from -6 to 6
- start_step: int32 [2], P('tm'), may hold values from 0 to 511
- velocity_x: float32 [256, 4096], P('space'), may hold values from -0.45 to 0.45
- velocity_y: float32 [256, 4096], P('space'), may hold values from -0.3 to 0.3
- amplitude: float32 [256, 4096], P('space'), may hold values from 0.2 to 1
- frequency: float32 [256, 4096], P('space'), may hold values from 0.3 to 2.5
- phase: float32 [256, 4096], P('space'), may hold values from -3.140625 to 3.140625
- sketch: float32 [64, 32], replicated, may hold values from -0.75 to 0.75
Outputs:
- piece: float32 [32, 256, 4096], P(None, 'space', 'tm')
- end_state: float32 [2, 2, 256, 4096], P('tm', None, 'space')
The draws below stay inside these ranges and needn't reach their ends.
All inputs are finite; a program needn't handle non-finite values.
Results may differ from the reference program's by a relative error of at most 0.0003.
Values sent between devices are 32-bit elements; how exact they have to be, the bound alone decides.
No kernel may reach another device: no remote copies, remote signals or barrier semaphores. Data moves between devices by JAX's collectives and lax.ppermute only.
A program may use at most 64 MiB of HBM per device.

```python
import math
import jax
import jax.numpy as jnp
from jax import lax

NY = 4096
STEPS = 16
RANK = 32
WIDE = 64
GROUPS = 2
NX = 256


def levels(rng, shape, cuts, least, high):
    factor_of = 1.0
    for dim, shards_of in cuts:
        heights = jax.random.uniform(jax.random.fold_in(jax.random.fold_in(rng, 6), dim), (shards_of,), jnp.float32, least / len(cuts), high / len(cuts))
        factor_of = factor_of * jnp.repeat(jnp.exp(heights), shape[dim] // shards_of).reshape((-1,) + (1,) * (len(shape) - 1 - dim))
    return factor_of


def scatter_about(key, extent, deviation, bound, split=(), kind=jnp.bfloat16):
    values = deviation * jax.random.normal(key, extent, jnp.float32)
    if split:
        values = values * levels(key, extent, split, -0.22, 0.18)
    return jnp.clip(values, -bound, bound).astype(kind)


def setup_inputs(seed: int = 0) -> dict:
    splits = jax.random.split(jax.random.key(seed), 9)
    return {
        "start_state": scatter_about(splits[0], (GROUPS, 2, NX, NY), 1.0, 6.0, ((0, 2), (2, 16)), jnp.float32),
        "start_step": jax.random.randint(splits[1], (GROUPS,), 0, 512).astype(jnp.int32),
        "velocity_x": jnp.clip(jax.random.uniform(splits[2], (NX, NY), jnp.float32, -0.45, 0.45) * levels(splits[2], (NX, NY), ((0, 16),), -0.4, 0.0), -0.45, 0.45),
        "velocity_y": jnp.clip(jax.random.uniform(splits[3], (NX, NY), jnp.float32, -0.3, 0.3) * levels(splits[3], (NX, NY), ((0, 16),), -0.4, 0.0), -0.3, 0.3),
        "amplitude": jnp.clip(jnp.exp(math.log(1.0) - 1.609438 * jax.random.uniform(splits[4], (NX, NY), jnp.float32) ** levels(splits[4], (NX, NY), ((0, 16),), -0.2, 0.2)), 0.2, 1.0),
        "frequency": jnp.clip(jnp.exp(math.log(2.5) - 2.1202635 * jax.random.uniform(splits[5], (NX, NY), jnp.float32) ** levels(splits[5], (NX, NY), ((0, 16),), -0.2, 0.2)), 0.3, 2.5),
        "phase": jnp.clip(jax.random.uniform(splits[6], (NX, NY), jnp.float32, -3.140625, 3.140625), -3.140625, 3.140625),
        "sketch": scatter_about(splits[7], (WIDE, RANK), WIDE ** -0.5, 0.75, (), jnp.float32),
    }


KAPPA = (0.06, 0.02)

def coefficients(gram, sketch):
    highest = lax.Precision.HIGHEST
    left = jnp.dot(sketch.T, gram, precision=highest)
    small = jnp.dot(left, sketch, precision=highest)
    lower = jnp.linalg.cholesky(small)
    proj = lax.linalg.triangular_solve(lower, left, left_side=True, lower=True)
    outer = jnp.dot(proj, proj.T, precision=highest)
    factor = jnp.linalg.cholesky(outer)
    mix_matrix = lax.linalg.triangular_solve(lower, factor, left_side=True, lower=True, transpose_a=True)
    return jnp.dot(sketch, mix_matrix, precision=highest)

def advance_step(state, padded, moment, velocity_x, velocity_y, amplitude, frequency, phase):
    east_side = padded[..., 2:, 1:-1]
    west_side = padded[..., :-2, 1:-1]
    north_side = padded[..., 1:-1, 2:]
    south_side = padded[..., 1:-1, :-2]
    kappa = jnp.array(KAPPA, jnp.float32).reshape(2, 1, 1)
    laplace_term = east_side + west_side + north_side + south_side - 4.0 * state
    transport = jnp.maximum(velocity_x, 0.0) * (state - west_side) + jnp.minimum(velocity_x, 0.0) * (east_side - state) + jnp.maximum(velocity_y, 0.0) * (state - south_side) + jnp.minimum(velocity_y, 0.0) * (north_side - state)
    angle = frequency * moment[:, None, None] + phase
    source = jnp.stack([amplitude * jnp.sin(angle), amplitude * jnp.cos(angle) * 0.5], axis=1)
    return state + kappa * laplace_term - transport + source

def reference(start_state, start_step, velocity_x, velocity_y, amplitude, frequency, phase, sketch):
    starts = start_step.astype(jnp.float32)

    def stepper(state, counter):
        wrapped = jnp.concatenate([state[..., -1:, :], state, state[..., :1, :]], axis=-2)
        padded = jnp.pad(wrapped, ((0, 0), (0, 0), (0, 0), (1, 1)))
        moment = starts + counter.astype(jnp.float32)
        fresh = advance_step(state, padded, moment, velocity_x, velocity_y, amplitude, frequency, phase)
        return (fresh, fresh)
    end_state, snaps = lax.scan(stepper, start_state, jnp.arange(STEPS, dtype=jnp.int32))
    groups = start_state.shape[0]
    snaps = jnp.transpose(snaps, (1, 2, 0, 3, 4)).reshape(groups, 2 * STEPS, NX, NY)
    pieces = [snaps[index] for index in range(groups)]
    while len(pieces) > 1:
        merged = []
        for index in range(len(pieces) // 2):
            joined = jnp.concatenate([pieces[2 * index], pieces[2 * index + 1]], axis=0)
            gram = jnp.einsum('cxy,dxy->cd', joined, joined, precision=lax.Precision.HIGHEST)
            coeff = coefficients(gram, sketch)
            merged.append(jnp.einsum('cxy,cr->rxy', joined, coeff, precision=lax.Precision.HIGHEST))
        pieces = merged
    return (pieces[0], end_state)
```

```python
import functools

import jax
import jax.numpy as jnp
import numpy as np
from jax import lax
from jax.experimental import pallas as pl
from jax.experimental.pallas import tpu as pltpu
from jax.sharding import PartitionSpec as P

STEPS = 16
KAPPA = (0.06, 0.02)
HIGHEST = lax.Precision.HIGHEST
AXES = ("space", "tm")
TILE = 128
GUARD = 8
BATCH = 4
VMEM = pl.BlockSpec(memory_space=pltpu.VMEM)
SMEM = pl.BlockSpec(memory_space=pltpu.SMEM)


def mm(a, b):
    return jnp.dot(a, b, precision=HIGHEST, preferred_element_type=jnp.float32)


def mm_nt(a, b):
    return lax.dot_general(
        a, b, (((1,), (1,)), ((), ())), precision=HIGHEST, preferred_element_type=jnp.float32
    )


def lanes_of(shape):
    return lax.broadcasted_iota(jnp.int32, shape, len(shape) - 1)


def pack_kernel(groups, block, step_ref, state_ref, vx, vy, amp, freq, phase, own_ref, *peer_refs):
    full = vx.shape[1]
    me = lax.axis_index("tm")
    start = step_ref[0].astype(jnp.float32)
    rows = vx.shape[0]
    lane = lanes_of((rows, TILE))

    def cut(read, target, write, is_state):
        first = target * block
        write(pl.ds(0, block), read(pl.ds(pl.multiple_of(first, TILE), block)))
        above = jnp.minimum(first + block, full - TILE)
        below = jnp.maximum(first - TILE, 0)
        high = read(pl.ds(pl.multiple_of(above, TILE), TILE))
        low = read(pl.ds(pl.multiple_of(below, TILE), TILE))
        high = jnp.where(target < groups - 1, high, 0.0)
        low = jnp.where(target > 0, low, 0.0)
        halo = jnp.where(lane < TILE // 2, high, low)
        if is_state:
            halo = jnp.where((lane >= TILE // 4) & (lane < 3 * TILE // 4), start, halo)
        write(pl.ds(block, TILE), halo)

    def writer(ref, index):
        def write(columns, value):
            ref[index, :, columns] = value

        return write

    for index, ref in enumerate((vx, vy, amp, freq, phase)):
        cut(lambda columns, ref=ref: ref[:, columns], me, writer(own_ref, index), False)
    for shift in range(groups):
        target = lax.rem(me + shift, groups)
        for field in range(2):
            if shift == 0:
                write = writer(own_ref, 5 + field)
            else:
                write = writer(peer_refs[shift - 1], field)
            cut(lambda columns, field=field: state_ref[0, field, :, columns], target, write, True)


def sin_cos(angle):
    turns = jnp.floor(angle * np.float32(2.0 / np.pi) + 0.5)
    r = angle - turns * np.float32(1.5703125)
    r = r - turns * np.float32(4.837512969970703125e-4)
    r = r - turns * np.float32(7.54978995489188216e-8)
    z = r * r
    sine = r + r * z * (
        np.float32(-1.6666654611e-1)
        + z * (np.float32(8.3321608736e-3) + z * np.float32(-1.9515295891e-4))
    )
    cosine = (
        1.0
        - 0.5 * z
        + z
        * z
        * (
            np.float32(4.166664568298827e-2)
            + z * (np.float32(-1.388731625493765e-3) + z * np.float32(2.443315711809948e-5))
        )
    )
    quadrant = turns.astype(jnp.int32)
    odd = (quadrant & 1) == 1
    s = jnp.where(odd, cosine, sine)
    c = jnp.where(odd, sine, cosine)
    s = jnp.where((quadrant & 2) == 2, -s, s)
    c = jnp.where(((quadrant + 1) & 2) == 2, -c, c)
    return s, c


def stencil_kernel(groups, halves, with_left, *refs):
    count = 3 * groups
    sources = [refs[3 * i : 3 * i + 3] for i in range(groups)]
    refs = refs[count:]
    if with_left:
        select_ref, fold_ref = refs[:2]
        refs = refs[2:]
        snap_ref, end_ref, left_ref = refs[:3]
        refs = refs[3:]
    else:
        snap_ref, end_ref = refs[:2]
        refs = refs[2:]
    qa, qb, xa, xb, twice, cw, ce, cs, cn, c0 = refs
    rows = sources[0][0].shape[1]
    block = sources[0][0].shape[2] - TILE
    length = block // halves
    tiles = length // TILE + 1
    subs = halves * groups * 2
    total = 3 * rows
    me = lax.axis_index("tm")

    sub = lax.broadcasted_iota(jnp.int32, (1, subs, TILE), 1)
    kappa = jnp.where((sub & 1) == 0, np.float32(KAPPA[0]), np.float32(KAPPA[1]))
    half_of = sub // (2 * groups)
    lane3 = lanes_of((1, subs, TILE))
    lowest = (me == 0) & (half_of == 0) & (lane3 >= TILE // 2)
    highest = (me == groups - 1) & (half_of == halves - 1) & (lane3 < TILE // 2)
    inside = jnp.where(lowest | highest, 0.0, 1.0).astype(jnp.float32)
    lane2 = lanes_of((8, TILE))

    for guard in (GUARD - 1, GUARD + total):
        qa[guard] = jnp.zeros(qa.shape[1:], jnp.float32)
        qb[guard] = jnp.zeros(qb.shape[1:], jnp.float32)

    def turned(parts):
        return jnp.swapaxes(jnp.stack(parts, axis=0), 0, 1)

    def prepare(place, base, tile, halo):
        def cut(ref, index, half):
            line = pl.ds(base, 8)
            if not halo:
                return ref[index, line, pl.ds(pl.multiple_of(half * length + tile * TILE, TILE), TILE)]
            above = (half + 1) * length
            below = half * length - TILE if half > 0 else block
            high = ref[index, line, above : above + TILE]
            if above == below:
                return high
            low = ref[index, line, below : below + TILE]
            return jnp.where(lane2 < TILE // 2, high, low)

        own = sources[0][place]
        starts, first, second, flow_x, flow_y, doubled = [], [], [], [], [], []
        for half in range(halves):
            vx, vy, amp, freq, phase = (cut(own, index, half) for index in range(5))
            sin_f, cos_f = sin_cos(freq)
            for group in range(groups):
                ref, at = sources[group][place], 5 if group == 0 else 0
                step = ref[at, pl.ds(base, 8), block : block + TILE][:, TILE // 2 : TILE // 2 + 1]
                s, c = sin_cos(freq * step + phase)
                s, c = amp * s, amp * c
                for field in range(2):
                    starts.append(cut(ref, at + field, half))
                    x, y = (s, c) if field == 0 else (0.5 * c, -0.5 * s)
                    first.append(x)
                    second.append(x * cos_f + y * sin_f)
                    flow_x.append(vx)
                    flow_y.append(vy)
                    doubled.append(2.0 * cos_f)
        where = pl.ds(place * rows + base, 8)
        columns = pl.ds(pl.multiple_of(tile * TILE, TILE), TILE)
        vx, vy = turned(flow_x), turned(flow_y)
        west = kappa + jnp.maximum(vx, 0.0)
        east = kappa - jnp.minimum(vx, 0.0)
        south = kappa + jnp.maximum(vy, 0.0)
        north = kappa - jnp.minimum(vy, 0.0)
        centre = 1.0 - (west + east + south + north)
        state, x0, x1 = turned(starts), turned(first), turned(second)
        if halo:
            west, east, south, north, centre, state, x0, x1 = (
                v * inside for v in (west, east, south, north, centre, state, x0, x1)
            )
        cw[where, :, columns] = west
        ce[where, :, columns] = east
        cs[where, :, columns] = south
        cn[where, :, columns] = north
        c0[where, :, columns] = centre
        xa[where, :, columns] = x0
        xb[where, :, columns] = x1
        twice[where, :, columns] = turned(doubled)
        qa[pl.ds(GUARD + place * rows + base, 8), :, columns] = state

    for place in range(3):

        def by_rows(number, carry, place=place):
            base = pl.multiple_of(number * 8, 8)

            def by_tiles(tile, inner):
                prepare(place, base, tile, False)
                return inner

            lax.fori_loop(0, tiles - 1, by_tiles, 0)
            prepare(place, base, tiles - 1, True)
            return carry

        lax.fori_loop(0, rows // 8, by_rows, 0)

    def advance(source, target, now, later, row, step, keep):
        for r in range(BATCH):
            x = row + r
            south = [
                pltpu.roll(source[GUARD + x, :, t * TILE : (t + 1) * TILE], 1, 1) for t in range(tiles)
            ]
            north = [
                pltpu.roll(source[GUARD + x, :, t * TILE : (t + 1) * TILE], TILE - 1, 1)
                for t in range(tiles)
            ]
            lane = lanes_of((subs, TILE))
            for t in range(tiles):
                cols = slice(t * TILE, (t + 1) * TILE)
                s = jnp.where(lane == 0, south[t - 1], south[t])
                n = jnp.where(lane == TILE - 1, north[(t + 1) % tiles], north[t])
                drive = now[x, :, cols]
                fresh = (
                    c0[x, :, cols] * source[GUARD + x, :, cols]
                    + cw[x, :, cols] * source[GUARD + x - 1, :, cols]
                    + ce[x, :, cols] * source[GUARD + x + 1, :, cols]
                    + cs[x, :, cols] * s
                    + cn[x, :, cols] * n
                    + drive
                )
                target[GUARD + x, :, cols] = fresh
                now[x, :, cols] = twice[x, :, cols] * later[x, :, cols] - drive
                if keep and t < tiles - 1:
                    snap_ref[x - rows, pl.ds(pl.multiple_of(step * subs, subs), subs), cols] = fresh

    def one(source, target, now, later, step):
        low = (step + 1) // BATCH
        high = (total - 1 - step + BATCH - 1) // BATCH

        def halo_rows(i, carry):
            advance(source, target, now, later, i * BATCH, step, False)
            return carry

        def own_rows(i, carry):
            advance(source, target, now, later, i * BATCH, step, True)
            return carry

        lax.fori_loop(low, rows // BATCH, halo_rows, 0)
        lax.fori_loop(rows // BATCH, 2 * rows // BATCH, own_rows, 0)
        lax.fori_loop(2 * rows // BATCH, high, halo_rows, 0)

    def pair(i, carry):
        one(qa, qb, xa, xb, 2 * i)
        one(qb, qa, xb, xa, 2 * i + 1)
        return carry

    lax.fori_loop(0, STEPS // 2, pair, 0)

    for base in range(0, rows, 8):
        for t in range(tiles - 1):
            cols = slice(t * TILE, (t + 1) * TILE)
            value = jnp.swapaxes(qa[GUARD + rows + base : GUARD + rows + base + 8, :, cols], 0, 1)
            for half in range(halves):
                for group in range(groups):
                    for field in range(2):
                        end_ref[
                            group, field, base : base + 8, half * length + t * TILE : half * length + (t + 1) * TILE
                        ] = value[half * groups * 2 + group * 2 + field]

    if with_left:
        width = STEPS * subs

        def add(x, gram):
            a = snap_ref[x]
            return gram + mm_nt(a, a)

        gram = lax.fori_loop(0, rows, add, jnp.zeros((width, width), jnp.float32))
        lane = lanes_of((1, width))
        left = jnp.zeros((select_ref.shape[0], width), jnp.float32)
        for half in range(halves):
            part = mm(select_ref[:, half * width : (half + 1) * width], gram)
            left = left + jnp.where((lane % subs) // (2 * groups) == half, part, 0.0)
        left_ref[...] = mm(left, fold_ref[...])


def eliminate(m, rank):
    row = lax.broadcasted_iota(jnp.int32, m.shape, 0)
    lane = lanes_of(m.shape)
    for k in range(rank):
        line = m[k : k + 1, :]
        pivot = m[k : k + 1, k : k + 1]
        column = m[:, k : k + 1] * (1.0 / pivot)
        m = m - jnp.where(row > k, column, 0.0) * line
    diagonal = jnp.sum(jnp.where(row == lane, m, 0.0), axis=1, keepdims=True)
    return m * lax.rsqrt(diagonal)


def merge_kernel(halves, subs, left_ref, spread_ref, unit_ref, expand_ref, snap_ref, out_ref):
    rank = left_ref.shape[0]
    wide = left_ref.shape[1]
    lane = lanes_of((rank, 128))
    whole = eliminate(mm(left_ref[...], spread_ref[...]) + unit_ref[...], rank)
    proj = jnp.where((lane >= rank) & (lane < rank + wide), whole, 0.0)
    outer = mm_nt(proj, proj)
    factor = eliminate(outer, rank)
    upper = jnp.where(
        lax.broadcasted_iota(jnp.int32, (rank, rank), 0) <= lanes_of((rank, rank)), factor, 0.0
    )
    mix = mm(upper, whole)
    width = snap_ref.shape[1]
    weights = jnp.concatenate(
        [mm(mix, expand_ref[:, half * width : (half + 1) * width]) for half in range(halves)], axis=0
    )
    rows = snap_ref.shape[0]
    length = snap_ref.shape[2]
    chunk = 256

    def columns(i, carry):
        at = pl.multiple_of(i * chunk, chunk)
        for base in range(0, rows, 8):
            parts = [mm(weights, snap_ref[base + x, :, pl.ds(at, chunk)]) for x in range(8)]
            for half in range(halves):
                for r in range(0, rank, 8):
                    first = half * rank + r
                    block = jnp.swapaxes(jnp.stack([p[first : first + 8] for p in parts], axis=0), 0, 1)
                    out_ref[r : r + 8, base : base + 8, pl.ds(pl.multiple_of(half * length + at, chunk), chunk)] = block
        return carry

    lax.fori_loop(0, length // chunk, columns, 0)


def shifted(value, along_space, along_tm):
    space, tm = lax.axis_size("space"), lax.axis_size("tm")
    moves = [
        (s * tm + t, (s + along_space) % space * tm + (t + along_tm) % tm)
        for s in range(space)
        for t in range(tm)
    ]
    return lax.ppermute(value, AXES, moves)


def turn(value, start):
    return lax.dynamic_slice_in_dim(jnp.concatenate([value, value]), start, value.shape[0], 0)


def total_of(value):
    size = lax.axis_size("space") * lax.axis_size("tm")
    if size & (size - 1):
        return lax.psum(value, AXES)
    bit = 1
    while bit < size:
        value = value + lax.ppermute(value, AXES, [(i, i ^ bit) for i in range(size)])
        bit *= 2
    return value


def coefficients(gram, sketch):
    left = jnp.dot(sketch.T, gram, precision=HIGHEST)
    small = jnp.dot(left, sketch, precision=HIGHEST)
    lower = jnp.linalg.cholesky(small)
    proj = lax.linalg.triangular_solve(lower, left, left_side=True, lower=True)
    outer = jnp.dot(proj, proj.T, precision=HIGHEST)
    factor = jnp.linalg.cholesky(outer)
    mix = lax.linalg.triangular_solve(lower, factor, left_side=True, lower=True, transpose_a=True)
    return jnp.dot(sketch, mix, precision=HIGHEST)


def merge_levels(pieces, sketch):
    while pieces.shape[0] > 1:
        count, columns, rows, length = pieces.shape
        joined = pieces.reshape(count // 2, 2 * columns, rows, length)
        gram = jnp.einsum("gcxy,gdxy->gcd", joined, joined, precision=HIGHEST)
        gram = lax.psum(gram, AXES)
        coeff = jax.vmap(coefficients, in_axes=(0, None))(gram, sketch)
        pieces = jnp.einsum("gcxy,gcr->grxy", joined, coeff, precision=HIGHEST)
    return pieces[0]


def body(start_state, start_step, velocity_x, velocity_y, amplitude, frequency, phase, sketch):
    groups = lax.axis_size("tm")
    me = lax.axis_index("tm")
    rows, full = velocity_x.shape
    block = full // groups
    halves = max(1, 8 // (2 * groups))
    subs = halves * groups * 2
    length = block // halves
    span = length + TILE
    width = STEPS * subs
    fast = groups == 2
    f32 = jnp.float32

    packed = pl.pallas_call(
        functools.partial(pack_kernel, groups, block),
        out_shape=[jax.ShapeDtypeStruct((7, rows, block + TILE), f32)]
        + [jax.ShapeDtypeStruct((2, rows, block + TILE), f32)] * (groups - 1),
        in_specs=[SMEM] + [VMEM] * 6,
        out_specs=[VMEM] * groups,
        name="pack",
    )(start_step, start_state, velocity_x, velocity_y, amplitude, frequency, phase)
    sources = [shifted(packed[0], 1, 0), packed[0], shifted(packed[0], -1, 0)]
    for shift in range(1, groups):
        sources += [shifted(packed[shift], move, shift) for move in (1, 0, -1)]

    extra = []
    if fast:
        column = np.arange(width)
        half_of = column % subs // (2 * groups)
        picks = np.zeros((groups, halves, 2 * STEPS * groups, width), np.float32)
        for member in range(groups):
            group = (member - column % (2 * groups) // 2) % groups
            index = group * 2 * STEPS + column % 2 * STEPS + column // subs
            picks[member, half_of, index, column] = 1.0
        pick = lax.dynamic_index_in_dim(jnp.asarray(picks), me, 0, keepdims=False)
        pick = jnp.concatenate([pick[half] for half in range(halves)], axis=1)
        select = jnp.dot(sketch.T, pick, precision=HIGHEST)
        fold = sum(pick[:, half * width : (half + 1) * width] for half in range(halves)).T
        rank, wide = sketch.shape[1], sketch.shape[0]
        spread = jnp.concatenate(
            [sketch, jnp.eye(wide, dtype=f32), jnp.zeros((wide, 128 - rank - wide), f32)], axis=1
        )
        unit = jnp.eye(rank, 128, 128 - rank, dtype=f32)
        expand = jnp.concatenate([jnp.zeros((128 - rank, halves * width), f32), select], axis=0)
        extra = [select, fold]

    outs = [
        jax.ShapeDtypeStruct((rows, width, length), f32),
        jax.ShapeDtypeStruct((groups, 2, rows, block), f32),
    ]
    if fast:
        outs.append(jax.ShapeDtypeStruct((sketch.shape[1], sketch.shape[0]), f32))
    grid_of = (3 * rows, subs, span)
    made = pl.pallas_call(
        functools.partial(stencil_kernel, groups, halves, fast),
        out_shape=outs,
        in_specs=[VMEM] * (len(sources) + len(extra)),
        out_specs=[VMEM] * len(outs),
        scratch_shapes=[pltpu.VMEM((3 * rows + 2 * GUARD, subs, span), f32)] * 2
        + [pltpu.VMEM(grid_of, f32)] * 8,
        compiler_params=pltpu.CompilerParams(vmem_limit_bytes=56 * 2**20),
        name="stencil",
    )(*sources, *extra)

    if fast:
        left = total_of(made[2])
        piece = pl.pallas_call(
            functools.partial(merge_kernel, halves, subs),
            out_shape=jax.ShapeDtypeStruct((rank, rows, block), f32),
            in_specs=[VMEM] * 5,
            out_specs=VMEM,
            compiler_params=pltpu.CompilerParams(vmem_limit_bytes=40 * 2**20),
            name="merge",
        )(left, spread, unit, expand, made[0])
    else:
        snaps = made[0].reshape(rows, STEPS, halves, groups, 2, length)
        snaps = jnp.transpose(snaps, (3, 4, 1, 0, 2, 5)).reshape(groups, 2 * STEPS, rows, block)
        snaps = turn(jnp.flip(snaps, 0), groups - 1 - me)
        piece = merge_levels(snaps, sketch)

    ends = [made[1][0]]
    for shift in range(1, groups):
        ends.append(shifted(made[1][shift], 0, groups - shift))
    if groups == 2:
        end_state = jnp.where(
            me == 0,
            jnp.concatenate([ends[0], ends[1]], axis=-1),
            jnp.concatenate([ends[1], ends[0]], axis=-1),
        )
    else:
        stacked = turn(jnp.stack(ends), groups - me)
        end_state = jnp.moveaxis(stacked, 0, -2).reshape(2, rows, full)
    return (piece, end_state[None])


def solution(mesh):
    placed = (
        P("tm", None, "space", None),
        P("tm"),
        P("space", None),
        P("space", None),
        P("space", None),
        P("space", None),
        P("space", None),
        P(),
    )
    return jax.shard_map(
        body,
        mesh=mesh,
        in_specs=placed,
        out_specs=(P(None, "space", "tm"), P("tm", None, "space", None)),
        check_vma=False,
    )
```

```python
import functools

import jax
import jax.numpy as jnp
import numpy as np
from jax import lax
from jax.experimental import pallas as pl
from jax.experimental.pallas import tpu as pltpu
from jax.sharding import PartitionSpec as P

STEPS = 16
KAPPA = (0.06, 0.02)
HIGHEST = lax.Precision.HIGHEST
AXES = ("space", "tm")
TILE = 128
GUARD = 8
BATCH = 4
OWN = 8
VMEM = pl.BlockSpec(memory_space=pltpu.VMEM)
SMEM = pl.BlockSpec(memory_space=pltpu.SMEM)


def mm(a, b):
    return jnp.dot(a, b, precision=HIGHEST, preferred_element_type=jnp.float32)


def mm_nt(a, b):
    return lax.dot_general(
        a, b, (((1,), (1,)), ((), ())), precision=HIGHEST, preferred_element_type=jnp.float32
    )


def lanes_of(shape):
    return lax.broadcasted_iota(jnp.int32, shape, len(shape) - 1)


def pack_kernel(groups, block, step_ref, state_ref, vx, vy, amp, freq, phase, own_ref, *peer_refs):
    full = vx.shape[1]
    me = lax.axis_index("tm")
    start = step_ref[0].astype(jnp.float32)
    rows = vx.shape[0]
    lane = lanes_of((rows, TILE))

    def cut(read, target, write, is_state):
        first = target * block
        write(pl.ds(0, block), read(pl.ds(pl.multiple_of(first, TILE), block)))
        above = jnp.minimum(first + block, full - TILE)
        below = jnp.maximum(first - TILE, 0)
        high = read(pl.ds(pl.multiple_of(above, TILE), TILE))
        low = read(pl.ds(pl.multiple_of(below, TILE), TILE))
        high = jnp.where(target < groups - 1, high, 0.0)
        low = jnp.where(target > 0, low, 0.0)
        halo = jnp.where(lane < TILE // 2, high, low)
        if is_state:
            halo = jnp.where((lane >= TILE // 4) & (lane < 3 * TILE // 4), start, halo)
        write(pl.ds(block, TILE), halo)

    def writer(ref, index):
        def write(columns, value):
            ref[index, :, columns] = value

        return write

    for index, ref in enumerate((vx, vy, amp, freq, phase)):
        cut(lambda columns, ref=ref: ref[:, columns], me, writer(own_ref, index), False)
    for shift in range(groups):
        target = lax.rem(me + shift, groups)
        for field in range(2):
            if shift == 0:
                write = writer(own_ref, 5 + field)
            else:
                write = writer(peer_refs[shift - 1], field)
            cut(lambda columns, field=field: state_ref[0, field, :, columns], target, write, True)


def sin_cos(angle):
    turns = jnp.floor(angle * np.float32(2.0 / np.pi) + 0.5)
    r = angle - turns * np.float32(1.5703125)
    r = r - turns * np.float32(4.837512969970703125e-4)
    r = r - turns * np.float32(7.54978995489188216e-8)
    z = r * r
    sine = r + r * z * (
        np.float32(-1.6666654611e-1)
        + z * (np.float32(8.3321608736e-3) + z * np.float32(-1.9515295891e-4))
    )
    cosine = (
        1.0
        - 0.5 * z
        + z
        * z
        * (
            np.float32(4.166664568298827e-2)
            + z * (np.float32(-1.388731625493765e-3) + z * np.float32(2.443315711809948e-5))
        )
    )
    quadrant = turns.astype(jnp.int32)
    odd = (quadrant & 1) == 1
    s = jnp.where(odd, cosine, sine)
    c = jnp.where(odd, sine, cosine)
    s = jnp.where((quadrant & 2) == 2, -s, s)
    c = jnp.where(((quadrant + 1) & 2) == 2, -c, c)
    return s, c


def stencil_kernel(groups, halves, with_left, *refs):
    count = 3 * groups
    sources = [refs[3 * i : 3 * i + 3] for i in range(groups)]
    refs = refs[count:]
    if with_left:
        select_ref, fold_ref = refs[:2]
        refs = refs[2:]
        snap_ref, end_ref, left_ref = refs[:3]
        refs = refs[3:]
    else:
        snap_ref, end_ref = refs[:2]
        refs = refs[2:]
    qa, qb, xa, xb, twice, cw, ce, cs, cn, c0, snap, sems = refs
    rows = sources[0][0].shape[1]
    block = sources[0][0].shape[2] - TILE
    length = block // halves
    tiles = length // TILE + 1
    subs = halves * groups * 2
    total = 3 * rows
    me = lax.axis_index("tm")

    sub = lax.broadcasted_iota(jnp.int32, (1, subs, TILE), 1)
    kappa = jnp.where((sub & 1) == 0, np.float32(KAPPA[0]), np.float32(KAPPA[1]))
    half_of = sub // (2 * groups)
    lane3 = lanes_of((1, subs, TILE))
    lowest = (me == 0) & (half_of == 0) & (lane3 >= TILE // 2)
    highest = (me == groups - 1) & (half_of == halves - 1) & (lane3 < TILE // 2)
    inside = jnp.where(lowest | highest, 0.0, 1.0).astype(jnp.float32)
    lane2 = lanes_of((8, TILE))

    for guard in (GUARD - 1, GUARD + total):
        qa[guard] = jnp.zeros(qa.shape[1:], jnp.float32)
        qb[guard] = jnp.zeros(qb.shape[1:], jnp.float32)

    def turned(parts):
        return jnp.swapaxes(jnp.stack(parts, axis=0), 0, 1)

    def prepare(place, base, tile, halo):
        def cut(ref, index, half):
            line = pl.ds(base, 8)
            if not halo:
                return ref[index, line, pl.ds(pl.multiple_of(half * length + tile * TILE, TILE), TILE)]
            above = (half + 1) * length
            below = half * length - TILE if half > 0 else block
            high = ref[index, line, above : above + TILE]
            if above == below:
                return high
            low = ref[index, line, below : below + TILE]
            return jnp.where(lane2 < TILE // 2, high, low)

        own = sources[0][place]
        starts, first, second, flow_x, flow_y, doubled = [], [], [], [], [], []
        for half in range(halves):
            vx, vy, amp, freq, phase = (cut(own, index, half) for index in range(5))
            sin_f, cos_f = sin_cos(freq)
            for group in range(groups):
                ref, at = sources[group][place], 5 if group == 0 else 0
                step = ref[at, pl.ds(base, 8), block : block + TILE][:, TILE // 2 : TILE // 2 + 1]
                s, c = sin_cos(freq * step + phase)
                s, c = amp * s, amp * c
                for field in range(2):
                    starts.append(cut(ref, at + field, half))
                    x, y = (s, c) if field == 0 else (0.5 * c, -0.5 * s)
                    first.append(x)
                    second.append(x * cos_f + y * sin_f)
                    flow_x.append(vx)
                    flow_y.append(vy)
                    doubled.append(2.0 * cos_f)
        where = pl.ds(place * rows + base, 8)
        columns = pl.ds(pl.multiple_of(tile * TILE, TILE), TILE)
        vx, vy = turned(flow_x), turned(flow_y)
        west = kappa + jnp.maximum(vx, 0.0)
        east = kappa - jnp.minimum(vx, 0.0)
        south = kappa + jnp.maximum(vy, 0.0)
        north = kappa - jnp.minimum(vy, 0.0)
        centre = 1.0 - (west + east + south + north)
        state, x0, x1 = turned(starts), turned(first), turned(second)
        if halo:
            west, east, south, north, centre, state, x0, x1 = (
                v * inside for v in (west, east, south, north, centre, state, x0, x1)
            )
        cw[where, :, columns] = west
        ce[where, :, columns] = east
        cs[where, :, columns] = south
        cn[where, :, columns] = north
        c0[where, :, columns] = centre
        xa[where, :, columns] = x0
        xb[where, :, columns] = x1
        twice[where, :, columns] = turned(doubled)
        qa[pl.ds(GUARD + place * rows + base, 8), :, columns] = state

    for place in range(3):

        def by_rows(number, carry, place=place):
            base = pl.multiple_of(number * 8, 8)

            def by_tiles(tile, inner):
                prepare(place, base, tile, False)
                return inner

            lax.fori_loop(0, tiles - 1, by_tiles, 0)
            prepare(place, base, tiles - 1, True)
            return carry

        lax.fori_loop(0, rows // 8, by_rows, 0)

    lane2s = lanes_of((subs, TILE))
    first_lane, last_lane = lane2s == 0, lane2s == TILE - 1

    def advance(source, target, now, later, row, count, step, keep):
        def tile_of(r, t):
            return source[GUARD + row + r, :, t * TILE : (t + 1) * TILE]

        held, up, down = {}, {}, {}

        def load(t):
            for r in range(-1, count + 1):
                held[r, t] = tile_of(r, t)
            for r in range(count):
                up[r, t] = pltpu.roll(held[r, t], 1, 1)
                down[r, t] = pltpu.roll(held[r, t], TILE - 1, 1)

        load(tiles - 1)
        load(0)
        for r in range(count):
            up[r, -1], down[r, tiles] = up[r, tiles - 1], down[r, 0]
        for t in range(tiles):
            if t + 1 < tiles - 1:
                load(t + 1)
            cols = slice(t * TILE, (t + 1) * TILE)
            for r in range(count):
                x = row + r
                south = jnp.where(first_lane, up[r, t - 1], up[r, t])
                north = jnp.where(last_lane, down[r, t + 1], down[r, t])
                drive = now[x, :, cols]
                fresh = (
                    (c0[x, :, cols] * held[r, t] + cw[x, :, cols] * held[r - 1, t])
                    + (ce[x, :, cols] * held[r + 1, t] + cs[x, :, cols] * south)
                    + (cn[x, :, cols] * north + drive)
                )
                target[GUARD + x, :, cols] = fresh
                now[x, :, cols] = twice[x, :, cols] * later[x, :, cols] - drive
                if keep and t < tiles - 1:
                    snap[x - rows, pl.ds(pl.multiple_of(step * subs, subs), subs), cols] = fresh

    def one(source, target, now, later, step):
        low = (step + 1) // BATCH
        high = (total - 1 - step + BATCH - 1) // BATCH

        def halo_rows(i, carry):
            advance(source, target, now, later, i * BATCH, BATCH, step, False)
            return carry

        def own_rows(i, carry):
            advance(source, target, now, later, i * OWN, OWN, step, True)
            return carry

        lax.fori_loop(low, rows // BATCH, halo_rows, 0)
        lax.fori_loop(rows // OWN, 2 * rows // OWN, own_rows, 0)
        copy_out(step).start()
        lax.fori_loop(2 * rows // BATCH, high, halo_rows, 0)

    def copy_out(step):
        part = pl.ds(pl.multiple_of(step * subs, subs), subs)
        return pltpu.make_async_copy(snap.at[:, part, :], snap_ref.at[:, part, :], sems.at[step])

    def pair(i, carry):
        one(qa, qb, xa, xb, 2 * i)
        one(qb, qa, xb, xa, 2 * i + 1)
        return carry

    lax.fori_loop(0, STEPS // 2, pair, 0)

    for base in range(0, rows, 8):
        for t in range(tiles - 1):
            cols = slice(t * TILE, (t + 1) * TILE)
            value = jnp.swapaxes(qa[GUARD + rows + base : GUARD + rows + base + 8, :, cols], 0, 1)
            for half in range(halves):
                for group in range(groups):
                    for field in range(2):
                        end_ref[
                            group, field, base : base + 8, half * length + t * TILE : half * length + (t + 1) * TILE
                        ] = value[half * groups * 2 + group * 2 + field]

    if with_left:
        width = STEPS * subs

        def add(x, total):
            a = snap[x]
            high = a.astype(jnp.bfloat16)
            low = (a - high.astype(jnp.float32)).astype(jnp.bfloat16)
            both = jnp.concatenate([high, low], axis=0)
            return total + lax.dot_general(
                both, both, (((1,), (1,)), ((), ())), preferred_element_type=jnp.float32
            )

        gram = lax.fori_loop(0, rows, add, jnp.zeros((2 * width, 2 * width), jnp.float32))
        gram = (gram[:width, :width] + gram[width:, width:]) + (gram[:width, width:] + gram[width:, :width])
        lane = lanes_of((1, width))
        left = jnp.zeros((select_ref.shape[0], width), jnp.float32)
        for half in range(halves):
            part = mm(select_ref[:, half * width : (half + 1) * width], gram)
            left = left + jnp.where((lane % subs) // (2 * groups) == half, part, 0.0)
        left_ref[...] = mm(left, fold_ref[...])

    def drained(step, carry):
        copy_out(step).wait()
        return carry

    lax.fori_loop(0, STEPS, drained, 0)


def eliminate(m, rank):
    row = lax.broadcasted_iota(jnp.int32, m.shape, 0)
    lane = lanes_of(m.shape)
    for k in range(0, rank, 2):
        line, after = m[k : k + 1, :], m[k + 1 : k + 2, :]
        column, beside = m[:, k : k + 1], m[:, k + 1 : k + 2]
        a, b, d = m[k : k + 1, k : k + 1], m[k + 1 : k + 2, k : k + 1], m[k + 1 : k + 2, k + 1 : k + 2]
        inverse = 1.0 / a
        ratio = b * inverse
        pivot = 1.0 / (d - ratio * b)
        after = after - ratio * line
        beside = (beside - ratio * column) * pivot
        m = (
            m
            - jnp.where(row > k, column * inverse, 0.0) * line
            - jnp.where(row > k + 1, beside, 0.0) * after
        )
    diagonal = jnp.sum(jnp.where(row == lane, m, 0.0), axis=1, keepdims=True)
    return m * lax.rsqrt(diagonal)


def in_two(x):
    high = x.astype(jnp.bfloat16)
    return high, (x - high.astype(jnp.float32)).astype(jnp.bfloat16)


CHUNK = 256


def merge_kernel(halves, left_ref, spread_ref, unit_ref, expand_ref, snap_ref, out_ref, snap, out, arrived, left_sems):
    rank = left_ref.shape[0]
    wide = left_ref.shape[1]
    rows, width, length = snap.shape
    parts = length // CHUNK

    def fetch(i):
        at = pl.ds(i * CHUNK, CHUNK)
        return pltpu.make_async_copy(snap_ref.at[:, :, at], snap.at[:, :, at], arrived.at[i])

    def store(i, half):
        at = pl.ds(half * length + i * CHUNK, CHUNK)
        return pltpu.make_async_copy(out.at[:, :, at], out_ref.at[:, :, at], left_sems.at[i, half])

    for i in range(parts):
        fetch(i).start()
    lane = lanes_of((rank, 128))
    whole = eliminate(mm(left_ref[...], spread_ref[...]) + unit_ref[...], rank)
    proj = jnp.where((lane >= rank) & (lane < rank + wide), whole, 0.0)
    outer = mm_nt(proj, proj)
    factor = eliminate(outer, rank)
    upper = jnp.where(
        lax.broadcasted_iota(jnp.int32, (rank, rank), 0) <= lanes_of((rank, rank)), factor, 0.0
    )
    mix = mm(upper, whole)
    weights = jnp.concatenate(
        [mm(mix, expand_ref[:, half * width : (half + 1) * width]) for half in range(halves)], axis=0
    )
    count = halves * rank
    high, low = in_two(weights)
    weights = jnp.concatenate(
        [jnp.concatenate([high, high], axis=1), jnp.concatenate([low, low], axis=1)], axis=0
    )
    for i in range(parts):
        fetch(i).wait()
        for base in range(0, rows, 8):
            made = []
            for x in range(base, base + 8):
                values = jnp.concatenate(in_two(snap[x, :, i * CHUNK : (i + 1) * CHUNK]), axis=0)
                both = jnp.dot(weights, values, preferred_element_type=jnp.float32)
                made.append(both[:count] + both[count:])
            for half in range(halves):
                at = half * length + i * CHUNK
                for r in range(0, rank, 8):
                    first = half * rank + r
                    block = jnp.stack([p[first : first + 8] for p in made], axis=0)
                    out[r : r + 8, base : base + 8, at : at + CHUNK] = jnp.swapaxes(block, 0, 1)
        for half in range(halves):
            store(i, half).start()
    for i in range(parts):
        for half in range(halves):
            store(i, half).wait()


def shifted(value, along_space, along_tm):
    space, tm = lax.axis_size("space"), lax.axis_size("tm")
    moves = [
        (s * tm + t, (s + along_space) % space * tm + (t + along_tm) % tm)
        for s in range(space)
        for t in range(tm)
    ]
    return lax.ppermute(value, AXES, moves)


def turn(value, start):
    return lax.dynamic_slice_in_dim(jnp.concatenate([value, value]), start, value.shape[0], 0)


def total_of(value):
    size = lax.axis_size("space") * lax.axis_size("tm")
    if size & (size - 1):
        return lax.psum(value, AXES)
    bit = 1
    while bit < size:
        value = value + lax.ppermute(value, AXES, [(i, i ^ bit) for i in range(size)])
        bit *= 2
    return value


def coefficients(gram, sketch):
    left = jnp.dot(sketch.T, gram, precision=HIGHEST)
    small = jnp.dot(left, sketch, precision=HIGHEST)
    lower = jnp.linalg.cholesky(small)
    proj = lax.linalg.triangular_solve(lower, left, left_side=True, lower=True)
    outer = jnp.dot(proj, proj.T, precision=HIGHEST)
    factor = jnp.linalg.cholesky(outer)
    mix = lax.linalg.triangular_solve(lower, factor, left_side=True, lower=True, transpose_a=True)
    return jnp.dot(sketch, mix, precision=HIGHEST)


def merge_levels(pieces, sketch):
    while pieces.shape[0] > 1:
        count, columns, rows, length = pieces.shape
        joined = pieces.reshape(count // 2, 2 * columns, rows, length)
        gram = jnp.einsum("gcxy,gdxy->gcd", joined, joined, precision=HIGHEST)
        gram = lax.psum(gram, AXES)
        coeff = jax.vmap(coefficients, in_axes=(0, None))(gram, sketch)
        pieces = jnp.einsum("gcxy,gcr->grxy", joined, coeff, precision=HIGHEST)
    return pieces[0]


def body(start_state, start_step, velocity_x, velocity_y, amplitude, frequency, phase, sketch):
    groups = lax.axis_size("tm")
    me = lax.axis_index("tm")
    rows, full = velocity_x.shape
    block = full // groups
    halves = max(1, 8 // (2 * groups))
    subs = halves * groups * 2
    length = block // halves
    span = length + TILE
    width = STEPS * subs
    fast = groups == 2
    f32 = jnp.float32

    packed = pl.pallas_call(
        functools.partial(pack_kernel, groups, block),
        out_shape=[jax.ShapeDtypeStruct((7, rows, block + TILE), f32)]
        + [jax.ShapeDtypeStruct((2, rows, block + TILE), f32)] * (groups - 1),
        in_specs=[SMEM] + [VMEM] * 6,
        out_specs=[VMEM] * groups,
        name="pack",
    )(start_step, start_state, velocity_x, velocity_y, amplitude, frequency, phase)
    sources = [shifted(packed[0], 1, 0), packed[0], shifted(packed[0], -1, 0)]
    for shift in range(1, groups):
        sources += [shifted(packed[shift], move, shift) for move in (1, 0, -1)]

    extra = []
    if fast:
        column = np.arange(width)
        half_of = column % subs // (2 * groups)
        picks = np.zeros((groups, halves, 2 * STEPS * groups, width), np.float32)
        for member in range(groups):
            group = (member - column % (2 * groups) // 2) % groups
            index = group * 2 * STEPS + column % 2 * STEPS + column // subs
            picks[member, half_of, index, column] = 1.0
        pick = lax.dynamic_index_in_dim(jnp.asarray(picks), me, 0, keepdims=False)
        pick = jnp.concatenate([pick[half] for half in range(halves)], axis=1)
        select = jnp.dot(sketch.T, pick, precision=HIGHEST)
        fold = sum(pick[:, half * width : (half + 1) * width] for half in range(halves)).T
        rank, wide = sketch.shape[1], sketch.shape[0]
        spread = jnp.concatenate(
            [sketch, jnp.eye(wide, dtype=f32), jnp.zeros((wide, 128 - rank - wide), f32)], axis=1
        )
        unit = jnp.eye(rank, 128, 128 - rank, dtype=f32)
        expand = jnp.concatenate([jnp.zeros((128 - rank, halves * width), f32), select], axis=0)
        extra = [select, fold]

    outs = [
        jax.ShapeDtypeStruct((rows, width, length), f32),
        jax.ShapeDtypeStruct((groups, 2, rows, block), f32),
    ]
    if fast:
        outs.append(jax.ShapeDtypeStruct((sketch.shape[1], sketch.shape[0]), f32))
    grid_of = (3 * rows, subs, span)
    made = pl.pallas_call(
        functools.partial(stencil_kernel, groups, halves, fast),
        out_shape=outs,
        in_specs=[VMEM] * (len(sources) + len(extra)),
        out_specs=[pl.BlockSpec(memory_space=pl.ANY)] + [VMEM] * (len(outs) - 1),
        scratch_shapes=[pltpu.VMEM((3 * rows + 2 * GUARD, subs, span), f32)] * 2
        + [pltpu.VMEM(grid_of, f32)] * 8
        + [pltpu.VMEM((rows, width, length), f32), pltpu.SemaphoreType.DMA((STEPS,))],
        compiler_params=pltpu.CompilerParams(vmem_limit_bytes=36 * 2**20),
        name="stencil",
    )(*sources, *extra)

    if fast:
        left = total_of(made[2])
        piece = pl.pallas_call(
            functools.partial(merge_kernel, halves),
            out_shape=jax.ShapeDtypeStruct((rank, rows, block), f32),
            in_specs=[VMEM] * 4 + [pl.BlockSpec(memory_space=pl.ANY)],
            out_specs=pl.BlockSpec(memory_space=pl.ANY),
            scratch_shapes=[
                pltpu.VMEM((rows, width, length), f32),
                pltpu.VMEM((rank, rows, block), f32),
                pltpu.SemaphoreType.DMA((length // CHUNK,)),
                pltpu.SemaphoreType.DMA((length // CHUNK, halves)),
            ],
            compiler_params=pltpu.CompilerParams(vmem_limit_bytes=24 * 2**20),
            name="merge",
        )(left, spread, unit, expand, made[0])
    else:
        snaps = made[0].reshape(rows, STEPS, halves, groups, 2, length)
        snaps = jnp.transpose(snaps, (3, 4, 1, 0, 2, 5)).reshape(groups, 2 * STEPS, rows, block)
        snaps = turn(jnp.flip(snaps, 0), groups - 1 - me)
        piece = merge_levels(snaps, sketch)

    ends = [made[1][0]]
    for shift in range(1, groups):
        ends.append(shifted(made[1][shift], 0, groups - shift))
    if groups == 2:
        end_state = jnp.where(
            me == 0,
            jnp.concatenate([ends[0], ends[1]], axis=-1),
            jnp.concatenate([ends[1], ends[0]], axis=-1),
        )
    else:
        stacked = turn(jnp.stack(ends), groups - me)
        end_state = jnp.moveaxis(stacked, 0, -2).reshape(2, rows, full)
    return (piece, end_state[None])


def solution(mesh):
    placed = (
        P("tm", None, "space", None),
        P("tm"),
        P("space", None),
        P("space", None),
        P("space", None),
        P("space", None),
        P("space", None),
        P(),
    )
    return jax.shard_map(
        body,
        mesh=mesh,
        in_specs=placed,
        out_specs=(P(None, "space", "tm"), P("tm", None, "space", None)),
        check_vma=False,
    )
```

```python
import functools

import jax
import jax.numpy as jnp
import numpy as np
from jax import lax
from jax.experimental import pallas as pl
from jax.experimental.pallas import tpu as pltpu
from jax.sharding import PartitionSpec as P

STEPS = 16
KAPPA = (0.06, 0.02)
HIGHEST = lax.Precision.HIGHEST
AXES = ("space", "tm")
TILE = 128
GUARD = 8
BATCH = 4
OWN = 8
VMEM = pl.BlockSpec(memory_space=pltpu.VMEM)
HBM = pl.BlockSpec(memory_space=pltpu.HBM)
SMEM = pl.BlockSpec(memory_space=pltpu.SMEM)


def mm(a, b):
    return jnp.dot(a, b, precision=HIGHEST, preferred_element_type=jnp.float32)


def mm_nt(a, b):
    return lax.dot_general(
        a, b, (((1,), (1,)), ((), ())), precision=HIGHEST, preferred_element_type=jnp.float32
    )


def lanes_of(shape):
    return lax.broadcasted_iota(jnp.int32, shape, len(shape) - 1)


def pack_kernel(groups, block, step_ref, state_ref, vx, vy, amp, freq, phase, own_ref, *peer_refs):
    full = vx.shape[1]
    me = lax.axis_index("tm")
    start = step_ref[0].astype(jnp.float32)
    rows = vx.shape[0]
    lane = lanes_of((rows, TILE))

    def cut(read, target, write, is_state):
        first = target * block
        write(pl.ds(0, block), read(pl.ds(pl.multiple_of(first, TILE), block)))
        above = jnp.minimum(first + block, full - TILE)
        below = jnp.maximum(first - TILE, 0)
        high = read(pl.ds(pl.multiple_of(above, TILE), TILE))
        low = read(pl.ds(pl.multiple_of(below, TILE), TILE))
        high = jnp.where(target < groups - 1, high, 0.0)
        low = jnp.where(target > 0, low, 0.0)
        halo = jnp.where(lane < TILE // 2, high, low)
        if is_state:
            halo = jnp.where((lane >= TILE // 4) & (lane < 3 * TILE // 4), start, halo)
        write(pl.ds(block, TILE), halo)

    def writer(ref, index):
        def write(columns, value):
            ref[index, :, columns] = value

        return write

    for index, ref in enumerate((vx, vy, amp, freq, phase)):
        cut(lambda columns, ref=ref: ref[:, columns], me, writer(own_ref, index), False)
    for shift in range(groups):
        target = lax.rem(me + shift, groups)
        for field in range(2):
            if shift == 0:
                write = writer(own_ref, 5 + field)
            else:
                write = writer(peer_refs[shift - 1], field)
            cut(lambda columns, field=field: state_ref[0, field, :, columns], target, write, True)


def sin_cos(angle):
    turns = jnp.floor(angle * np.float32(2.0 / np.pi) + 0.5)
    r = angle - turns * np.float32(1.5703125)
    r = r - turns * np.float32(4.837512969970703125e-4)
    r = r - turns * np.float32(7.54978995489188216e-8)
    z = r * r
    sine = r + r * z * (
        np.float32(-1.6666654611e-1)
        + z * (np.float32(8.3321608736e-3) + z * np.float32(-1.9515295891e-4))
    )
    cosine = (
        1.0
        - 0.5 * z
        + z
        * z
        * (
            np.float32(4.166664568298827e-2)
            + z * (np.float32(-1.388731625493765e-3) + z * np.float32(2.443315711809948e-5))
        )
    )
    quadrant = turns.astype(jnp.int32)
    odd = (quadrant & 1) == 1
    s = jnp.where(odd, cosine, sine)
    c = jnp.where(odd, sine, cosine)
    s = jnp.where((quadrant & 2) == 2, -s, s)
    c = jnp.where(((quadrant + 1) & 2) == 2, -c, c)
    return s, c


def stencil_kernel(groups, halves, with_left, *refs):
    count = 3 * groups
    sources = [refs[3 * i : 3 * i + 3] for i in range(groups)]
    refs = refs[count:]
    if with_left:
        select_ref, fold_ref = refs[:2]
        refs = refs[2:]
        snap_ref, end_ref, left_ref = refs[:3]
        refs = refs[3:]
    else:
        snap_ref, end_ref = refs[:2]
        refs = refs[2:]
    qa, qb, xa, xb, twice, cw, ce, cs, cn, c0, snap, sems = refs
    rows = sources[0][0].shape[1]
    block = sources[0][0].shape[2] - TILE
    length = block // halves
    tiles = length // TILE + 1
    subs = halves * groups * 2
    total = 3 * rows
    me = lax.axis_index("tm")

    sub = lax.broadcasted_iota(jnp.int32, (1, subs, TILE), 1)
    kappa = jnp.where((sub & 1) == 0, np.float32(KAPPA[0]), np.float32(KAPPA[1]))
    half_of = sub // (2 * groups)
    lane3 = lanes_of((1, subs, TILE))
    lowest = (me == 0) & (half_of == 0) & (lane3 >= TILE // 2)
    highest = (me == groups - 1) & (half_of == halves - 1) & (lane3 < TILE // 2)
    inside = jnp.where(lowest | highest, 0.0, 1.0).astype(jnp.float32)
    lane2 = lanes_of((8, TILE))

    for guard in (GUARD - 1, GUARD + total):
        qa[guard] = jnp.zeros(qa.shape[1:], jnp.float32)
        qb[guard] = jnp.zeros(qb.shape[1:], jnp.float32)

    def turned(parts):
        return jnp.swapaxes(jnp.stack(parts, axis=0), 0, 1)

    def prepare(place, base, tile, halo):
        def cut(ref, index, half):
            line = pl.ds(base, 8)
            if not halo:
                return ref[index, line, pl.ds(pl.multiple_of(half * length + tile * TILE, TILE), TILE)]
            above = (half + 1) * length
            below = half * length - TILE if half > 0 else block
            high = ref[index, line, above : above + TILE]
            if above == below:
                return high
            low = ref[index, line, below : below + TILE]
            return jnp.where(lane2 < TILE // 2, high, low)

        own = sources[0][place]
        starts, first, second, flow_x, flow_y, doubled = [], [], [], [], [], []
        for half in range(halves):
            vx, vy, amp, freq, phase = (cut(own, index, half) for index in range(5))
            sin_f, cos_f = sin_cos(freq)
            for group in range(groups):
                ref, at = sources[group][place], 5 if group == 0 else 0
                step = ref[at, pl.ds(base, 8), block : block + TILE][:, TILE // 2 : TILE // 2 + 1]
                s, c = sin_cos(freq * step + phase)
                s, c = amp * s, amp * c
                for field in range(2):
                    starts.append(cut(ref, at + field, half))
                    x, y = (s, c) if field == 0 else (0.5 * c, -0.5 * s)
                    first.append(x)
                    second.append(x * cos_f + y * sin_f)
                    flow_x.append(vx)
                    flow_y.append(vy)
                    doubled.append(2.0 * cos_f)
        where = pl.ds(place * rows + base, 8)
        columns = pl.ds(pl.multiple_of(tile * TILE, TILE), TILE)
        vx, vy = turned(flow_x), turned(flow_y)
        west = kappa + jnp.maximum(vx, 0.0)
        east = kappa - jnp.minimum(vx, 0.0)
        south = kappa + jnp.maximum(vy, 0.0)
        north = kappa - jnp.minimum(vy, 0.0)
        centre = 1.0 - (west + east + south + north)
        state, x0, x1 = turned(starts), turned(first), turned(second)
        if halo:
            west, east, south, north, centre, state, x0, x1 = (
                v * inside for v in (west, east, south, north, centre, state, x0, x1)
            )
        cw[where, :, columns] = west
        ce[where, :, columns] = east
        cs[where, :, columns] = south
        cn[where, :, columns] = north
        c0[where, :, columns] = centre
        xa[where, :, columns] = x0
        xb[where, :, columns] = x1
        twice[where, :, columns] = turned(doubled)
        qa[pl.ds(GUARD + place * rows + base, 8), :, columns] = state

    for place in range(3):

        def by_rows(number, carry, place=place):
            base = pl.multiple_of(number * 8, 8)

            def by_tiles(tile, inner):
                prepare(place, base, tile, False)
                return inner

            lax.fori_loop(0, tiles - 1, by_tiles, 0)
            prepare(place, base, tiles - 1, True)
            return carry

        lax.fori_loop(0, rows // 8, by_rows, 0)

    lane2s = lanes_of((subs, TILE))
    first_lane, last_lane = lane2s == 0, lane2s == TILE - 1

    def advance(source, target, now, later, row, count, step, keep):
        def tile_of(r, t):
            return source[GUARD + row + r, :, t * TILE : (t + 1) * TILE]

        held, up, down = {}, {}, {}

        def load(t):
            for r in range(-1, count + 1):
                held[r, t] = tile_of(r, t)
            for r in range(count):
                up[r, t] = pltpu.roll(held[r, t], 1, 1)
                down[r, t] = pltpu.roll(held[r, t], TILE - 1, 1)

        load(tiles - 1)
        load(0)
        for r in range(count):
            up[r, -1], down[r, tiles] = up[r, tiles - 1], down[r, 0]
        for t in range(tiles):
            if t + 1 < tiles - 1:
                load(t + 1)
            cols = slice(t * TILE, (t + 1) * TILE)
            for r in range(count):
                x = row + r
                south = jnp.where(first_lane, up[r, t - 1], up[r, t])
                north = jnp.where(last_lane, down[r, t + 1], down[r, t])
                drive = now[x, :, cols]
                fresh = (
                    (c0[x, :, cols] * held[r, t] + cw[x, :, cols] * held[r - 1, t])
                    + (ce[x, :, cols] * held[r + 1, t] + cs[x, :, cols] * south)
                    + (cn[x, :, cols] * north + drive)
                )
                target[GUARD + x, :, cols] = fresh
                now[x, :, cols] = twice[x, :, cols] * later[x, :, cols] - drive
                if keep and t < tiles - 1:
                    snap[x - rows, pl.ds(pl.multiple_of(step * subs, subs), subs), cols] = fresh

    def one(source, target, now, later, step):
        low = (step + 1) // BATCH
        high = (total - 1 - step + BATCH - 1) // BATCH

        def halo_rows(i, carry):
            advance(source, target, now, later, i * BATCH, BATCH, step, False)
            return carry

        def own_rows(i, carry):
            advance(source, target, now, later, i * OWN, OWN, step, True)
            return carry

        lax.fori_loop(low, rows // BATCH, halo_rows, 0)
        lax.fori_loop(rows // OWN, 2 * rows // OWN, own_rows, 0)
        copy_out(step).start()
        lax.fori_loop(2 * rows // BATCH, high, halo_rows, 0)

    def copy_out(step):
        part = pl.ds(pl.multiple_of(step * subs, subs), subs)
        return pltpu.make_async_copy(snap.at[:, part, :], snap_ref.at[:, part, :], sems.at[step])

    def pair(i, carry):
        one(qa, qb, xa, xb, 2 * i)
        one(qb, qa, xb, xa, 2 * i + 1)
        return carry

    lax.fori_loop(0, STEPS // 2, pair, 0)

    for base in range(0, rows, 8):
        for t in range(tiles - 1):
            cols = slice(t * TILE, (t + 1) * TILE)
            value = jnp.swapaxes(qa[GUARD + rows + base : GUARD + rows + base + 8, :, cols], 0, 1)
            for half in range(halves):
                for group in range(groups):
                    for field in range(2):
                        end_ref[
                            group, field, base : base + 8, half * length + t * TILE : half * length + (t + 1) * TILE
                        ] = value[half * groups * 2 + group * 2 + field]

    if with_left:
        width = STEPS * subs

        def add(x, total):
            a = snap[x]
            high = a.astype(jnp.bfloat16)
            low = (a - high.astype(jnp.float32)).astype(jnp.bfloat16)
            both = jnp.concatenate([high, low], axis=0)
            return total + lax.dot_general(
                both, both, (((1,), (1,)), ((), ())), preferred_element_type=jnp.float32
            )

        gram = lax.fori_loop(0, rows, add, jnp.zeros((2 * width, 2 * width), jnp.float32))
        gram = (gram[:width, :width] + gram[width:, width:]) + (gram[:width, width:] + gram[width:, :width])
        lane = lanes_of((1, width))
        left = jnp.zeros((select_ref.shape[0], width), jnp.float32)
        for half in range(halves):
            part = mm(select_ref[:, half * width : (half + 1) * width], gram)
            left = left + jnp.where((lane % subs) // (2 * groups) == half, part, 0.0)
        left_ref[...] = mm(left, fold_ref[...])

    def drained(step, carry):
        copy_out(step).wait()
        return carry

    lax.fori_loop(0, STEPS, drained, 0)


def eliminate(m, rank):
    row = lax.broadcasted_iota(jnp.int32, m.shape, 0)
    lane = lanes_of(m.shape)
    for k in range(0, rank, 2):
        line, after = m[k : k + 1, :], m[k + 1 : k + 2, :]
        column = jnp.broadcast_to(m[:, k : k + 1], m.shape)
        beside = jnp.broadcast_to(m[:, k + 1 : k + 2], m.shape)
        a, b, d = column[k : k + 1], column[k + 1 : k + 2], beside[k + 1 : k + 2]
        inverse = 1.0 / a
        ratio = b * inverse
        pivot = 1.0 / (d - ratio * b)
        after = after - ratio * line
        beside = (beside - ratio * column) * pivot
        m = (
            m
            - jnp.where(row > k, column * inverse, 0.0) * line
            - jnp.where(row > k + 1, beside, 0.0) * after
        )
    diagonal = jnp.sum(jnp.where(row == lane, m, 0.0), axis=1, keepdims=True)
    return m * lax.rsqrt(diagonal)


def in_two(x):
    high = x.astype(jnp.bfloat16)
    return high, (x - high.astype(jnp.float32)).astype(jnp.bfloat16)


CHUNK = 256


def merge_kernel(halves, left_ref, spread_ref, unit_ref, expand_ref, snap_ref, out_ref, snap, out, arrived, left_sems):
    rank = left_ref.shape[0]
    wide = left_ref.shape[1]
    rows, width, length = snap.shape
    parts = length // CHUNK

    def fetch(i):
        at = pl.ds(i * CHUNK, CHUNK)
        return pltpu.make_async_copy(snap_ref.at[:, :, at], snap.at[:, :, at], arrived.at[i])

    def store(i, half):
        at = pl.ds(half * length + i * CHUNK, CHUNK)
        return pltpu.make_async_copy(out.at[:, :, at], out_ref.at[:, :, at], left_sems.at[i, half])

    for i in range(parts):
        fetch(i).start()
    lane = lanes_of((rank, 128))
    whole = eliminate(mm(left_ref[...], spread_ref[...]) + unit_ref[...], rank)
    proj = jnp.where((lane >= rank) & (lane < rank + wide), whole, 0.0)
    outer = mm_nt(proj, proj)
    factor = eliminate(outer, rank)
    upper = jnp.where(
        lax.broadcasted_iota(jnp.int32, (rank, rank), 0) <= lanes_of((rank, rank)), factor, 0.0
    )
    mix = mm(upper, whole)
    weights = jnp.concatenate(
        [mm(mix, expand_ref[:, half * width : (half + 1) * width]) for half in range(halves)], axis=0
    )
    count = halves * rank
    high, low = in_two(weights)
    weights = jnp.concatenate(
        [jnp.concatenate([high, high], axis=1), jnp.concatenate([low, low], axis=1)], axis=0
    )
    for i in range(parts):
        fetch(i).wait()
        for base in range(0, rows, 8):
            made = []
            for x in range(base, base + 8):
                values = jnp.concatenate(in_two(snap[x, :, i * CHUNK : (i + 1) * CHUNK]), axis=0)
                both = jnp.dot(weights, values, preferred_element_type=jnp.float32)
                made.append(both[:count] + both[count:])
            for half in range(halves):
                at = half * length + i * CHUNK
                for r in range(0, rank, 8):
                    first = half * rank + r
                    block = jnp.stack([p[first : first + 8] for p in made], axis=0)
                    out[r : r + 8, base : base + 8, at : at + CHUNK] = jnp.swapaxes(block, 0, 1)
        for half in range(halves):
            store(i, half).start()
    for i in range(parts):
        for half in range(halves):
            store(i, half).wait()


def shifted(value, along_space, along_tm):
    space, tm = lax.axis_size("space"), lax.axis_size("tm")
    moves = [
        (s * tm + t, (s + along_space) % space * tm + (t + along_tm) % tm)
        for s in range(space)
        for t in range(tm)
    ]
    return lax.ppermute(value, AXES, moves)


def turn(value, start):
    return lax.dynamic_slice_in_dim(jnp.concatenate([value, value]), start, value.shape[0], 0)


def total_of(value):
    size = lax.axis_size("space") * lax.axis_size("tm")
    if size & (size - 1):
        return lax.psum(value, AXES)
    bit = 1
    while bit < size:
        value = value + lax.ppermute(value, AXES, [(i, i ^ bit) for i in range(size)])
        bit *= 2
    return value


def coefficients(gram, sketch):
    left = jnp.dot(sketch.T, gram, precision=HIGHEST)
    small = jnp.dot(left, sketch, precision=HIGHEST)
    lower = jnp.linalg.cholesky(small)
    proj = lax.linalg.triangular_solve(lower, left, left_side=True, lower=True)
    outer = jnp.dot(proj, proj.T, precision=HIGHEST)
    factor = jnp.linalg.cholesky(outer)
    mix = lax.linalg.triangular_solve(lower, factor, left_side=True, lower=True, transpose_a=True)
    return jnp.dot(sketch, mix, precision=HIGHEST)


def merge_levels(pieces, sketch):
    while pieces.shape[0] > 1:
        count, columns, rows, length = pieces.shape
        joined = pieces.reshape(count // 2, 2 * columns, rows, length)
        gram = jnp.einsum("gcxy,gdxy->gcd", joined, joined, precision=HIGHEST)
        gram = lax.psum(gram, AXES)
        coeff = jax.vmap(coefficients, in_axes=(0, None))(gram, sketch)
        pieces = jnp.einsum("gcxy,gcr->grxy", joined, coeff, precision=HIGHEST)
    return pieces[0]


def body(start_state, start_step, velocity_x, velocity_y, amplitude, frequency, phase, sketch):
    groups = lax.axis_size("tm")
    me = lax.axis_index("tm")
    rows, full = velocity_x.shape
    block = full // groups
    halves = max(1, 8 // (2 * groups))
    subs = halves * groups * 2
    length = block // halves
    span = length + TILE
    width = STEPS * subs
    fast = groups == 2
    f32 = jnp.float32

    packed = pl.pallas_call(
        functools.partial(pack_kernel, groups, block),
        out_shape=[jax.ShapeDtypeStruct((7, rows, block + TILE), f32)]
        + [jax.ShapeDtypeStruct((2, rows, block + TILE), f32)] * (groups - 1),
        in_specs=[SMEM] + [VMEM] * 6,
        out_specs=[VMEM] * groups,
        name="pack",
    )(start_step, start_state, velocity_x, velocity_y, amplitude, frequency, phase)
    sources = [shifted(packed[0], 1, 0), packed[0], shifted(packed[0], -1, 0)]
    for shift in range(1, groups):
        sources += [shifted(packed[shift], move, shift) for move in (1, 0, -1)]

    extra = []
    if fast:
        column = np.arange(width)
        half_of = column % subs // (2 * groups)
        picks = np.zeros((groups, halves, 2 * STEPS * groups, width), np.float32)
        for member in range(groups):
            group = (member - column % (2 * groups) // 2) % groups
            index = group * 2 * STEPS + column % 2 * STEPS + column // subs
            picks[member, half_of, index, column] = 1.0
        pick = lax.dynamic_index_in_dim(jnp.asarray(picks), me, 0, keepdims=False)
        pick = jnp.concatenate([pick[half] for half in range(halves)], axis=1)
        select = jnp.dot(sketch.T, pick, precision=HIGHEST)
        fold = sum(pick[:, half * width : (half + 1) * width] for half in range(halves)).T
        rank, wide = sketch.shape[1], sketch.shape[0]
        spread = jnp.concatenate(
            [sketch, jnp.eye(wide, dtype=f32), jnp.zeros((wide, 128 - rank - wide), f32)], axis=1
        )
        unit = jnp.eye(rank, 128, 128 - rank, dtype=f32)
        expand = jnp.concatenate([jnp.zeros((128 - rank, halves * width), f32), select], axis=0)
        extra = [select, fold]

    outs = [
        pltpu.HBM((rows, width, length), f32),
        jax.ShapeDtypeStruct((groups, 2, rows, block), f32),
    ]
    if fast:
        outs.append(jax.ShapeDtypeStruct((sketch.shape[1], sketch.shape[0]), f32))
    grid_of = (3 * rows, subs, span)
    made = pl.pallas_call(
        functools.partial(stencil_kernel, groups, halves, fast),
        out_shape=outs,
        in_specs=[VMEM] * (len(sources) + len(extra)),
        out_specs=[HBM] + [VMEM] * (len(outs) - 1),
        scratch_shapes=[pltpu.VMEM((3 * rows + 2 * GUARD, subs, span), f32)] * 2
        + [pltpu.VMEM(grid_of, f32)] * 8
        + [pltpu.VMEM((rows, width, length), f32), pltpu.SemaphoreType.DMA((STEPS,))],
        compiler_params=pltpu.CompilerParams(vmem_limit_bytes=36 * 2**20),
        name="stencil",
    )(*sources, *extra)

    if fast:
        left = total_of(made[2])
        piece = pl.pallas_call(
            functools.partial(merge_kernel, halves),
            out_shape=jax.ShapeDtypeStruct((rank, rows, block), f32),
            in_specs=[VMEM] * 4 + [HBM],
            out_specs=HBM,
            scratch_shapes=[
                pltpu.VMEM((rows, width, length), f32),
                pltpu.VMEM((rank, rows, block), f32),
                pltpu.SemaphoreType.DMA((length // CHUNK,)),
                pltpu.SemaphoreType.DMA((length // CHUNK, halves)),
            ],
            compiler_params=pltpu.CompilerParams(vmem_limit_bytes=54 * 2**20),
            name="merge",
        )(left, spread, unit, expand, made[0])
    else:
        snaps = made[0].reshape(rows, STEPS, halves, groups, 2, length)
        snaps = jnp.transpose(snaps, (3, 4, 1, 0, 2, 5)).reshape(groups, 2 * STEPS, rows, block)
        snaps = turn(jnp.flip(snaps, 0), groups - 1 - me)
        piece = merge_levels(snaps, sketch)

    ends = [made[1][0]]
    for shift in range(1, groups):
        ends.append(shifted(made[1][shift], 0, groups - shift))
    if groups == 2:
        end_state = jnp.where(
            me == 0,
            jnp.concatenate([ends[0], ends[1]], axis=-1),
            jnp.concatenate([ends[1], ends[0]], axis=-1),
        )
    else:
        stacked = turn(jnp.stack(ends), groups - me)
        end_state = jnp.moveaxis(stacked, 0, -2).reshape(2, rows, full)
    return (piece, end_state[None])


def solution(mesh):
    placed = (
        P("tm", None, "space", None),
        P("tm"),
        P("space", None),
        P("space", None),
        P("space", None),
        P("space", None),
        P("space", None),
        P(),
    )
    return jax.shard_map(
        body,
        mesh=mesh,
        in_specs=placed,
        out_specs=(P(None, "space", "tm"), P("tm", None, "space", None)),
        check_vma=False,
    )
```

```python
import functools

import jax
import jax.numpy as jnp
import numpy as np
from jax import lax
from jax.experimental import pallas as pl
from jax.experimental.pallas import tpu as pltpu
from jax.sharding import PartitionSpec as P

STEPS = 16
KAPPA = (0.06, 0.02)
HIGHEST = lax.Precision.HIGHEST
AXES = ("space", "tm")
TILE = 128
GUARD = 8
BATCH = 4
OWN = 8
REACH = STEPS // 2
VMEM = pl.BlockSpec(memory_space=pltpu.VMEM)
HBM = pl.BlockSpec(memory_space=pltpu.HBM)
SMEM = pl.BlockSpec(memory_space=pltpu.SMEM)


def mm(a, b):
    return jnp.dot(a, b, precision=HIGHEST, preferred_element_type=jnp.float32)


def mm_nt(a, b):
    return lax.dot_general(
        a, b, (((1,), (1,)), ((), ())), precision=HIGHEST, preferred_element_type=jnp.float32
    )


def lanes_of(shape):
    return lax.broadcasted_iota(jnp.int32, shape, len(shape) - 1)


def pack_kernel(groups, block, step_ref, state_ref, vx, vy, amp, freq, phase, *out_refs):
    full = vx.shape[1]
    me = lax.axis_index("tm")
    start = step_ref[0].astype(jnp.float32)
    rows = vx.shape[0]
    lane = lanes_of((rows, TILE))

    def cut(read, target, write, is_state):
        first = target * block
        write(pl.ds(0, block), read(pl.ds(pl.multiple_of(first, TILE), block)))
        above = jnp.minimum(first + block, full - TILE)
        below = jnp.maximum(first - TILE, 0)
        high = read(pl.ds(pl.multiple_of(above, TILE), TILE))
        low = read(pl.ds(pl.multiple_of(below, TILE), TILE))
        high = jnp.where(target < groups - 1, high, 0.0)
        low = jnp.where(target > 0, low, 0.0)
        halo = jnp.where(lane < TILE // 2, high, low)
        if is_state:
            halo = jnp.where((lane >= TILE // 4) & (lane < 3 * TILE // 4), start, halo)
        write(pl.ds(block, TILE), halo)

    def writer(group, index):
        low, every, high = out_refs[3 * group : 3 * group + 3]

        def write(columns, value):
            low[index, :, columns] = value[:REACH]
            every[index, :, columns] = value
            high[index, :, columns] = value[rows - REACH :]

        return write

    for index, ref in enumerate((vx, vy, amp, freq, phase)):
        cut(lambda columns, ref=ref: ref[:, columns], me, writer(0, index), False)
    for shift in range(groups):
        target = lax.rem(me + shift, groups)
        for field in range(2):
            write = writer(shift, 5 + field if shift == 0 else field)
            cut(lambda columns, field=field: state_ref[0, field, :, columns], target, write, True)


def sin_cos(angle):
    turns = jnp.floor(angle * np.float32(2.0 / np.pi) + 0.5)
    r = angle - turns * np.float32(1.5703125)
    r = r - turns * np.float32(4.837512969970703125e-4)
    r = r - turns * np.float32(7.54978995489188216e-8)
    z = r * r
    sine = r + r * z * (
        np.float32(-1.6666654611e-1)
        + z * (np.float32(8.3321608736e-3) + z * np.float32(-1.9515295891e-4))
    )
    cosine = (
        1.0
        - 0.5 * z
        + z
        * z
        * (
            np.float32(4.166664568298827e-2)
            + z * (np.float32(-1.388731625493765e-3) + z * np.float32(2.443315711809948e-5))
        )
    )
    quadrant = turns.astype(jnp.int32)
    odd = (quadrant & 1) == 1
    s = jnp.where(odd, cosine, sine)
    c = jnp.where(odd, sine, cosine)
    s = jnp.where((quadrant & 2) == 2, -s, s)
    c = jnp.where(((quadrant + 1) & 2) == 2, -c, c)
    return s, c


def run_phase(grid, rows, snap, snap_ref, sems, keep_drift):
    qa, qb, xa, xb, twice, cw, ce, cs, cn, c0 = grid
    subs = qa.shape[1]
    tiles = qa.shape[2] // TILE
    total = rows + 2 * REACH

    for guard in (GUARD - 1, GUARD + total):
        qa[guard] = jnp.zeros(qa.shape[1:], jnp.float32)
        qb[guard] = jnp.zeros(qb.shape[1:], jnp.float32)

    lane2s = lanes_of((subs, TILE))
    first_lane, last_lane = lane2s == 0, lane2s == TILE - 1

    def advance(source, target, now, later, row, count, step, keep):
        def tile_of(r, t):
            return source[GUARD + row + r, :, t * TILE : (t + 1) * TILE]

        held, up, down = {}, {}, {}

        def load(t):
            for r in range(-1, count + 1):
                held[r, t] = tile_of(r, t)
            for r in range(count):
                up[r, t] = pltpu.roll(held[r, t], 1, 1)
                down[r, t] = pltpu.roll(held[r, t], TILE - 1, 1)

        load(tiles - 1)
        load(0)
        for r in range(count):
            up[r, -1], down[r, tiles] = up[r, tiles - 1], down[r, 0]
        for t in range(tiles):
            if t + 1 < tiles - 1:
                load(t + 1)
            cols = slice(t * TILE, (t + 1) * TILE)
            for r in range(count):
                x = row + r
                south = jnp.where(first_lane, up[r, t - 1], up[r, t])
                north = jnp.where(last_lane, down[r, t + 1], down[r, t])
                drive = now[x, :, cols]
                fresh = (
                    (c0[x, :, cols] * held[r, t] + cw[x, :, cols] * held[r - 1, t])
                    + (ce[x, :, cols] * held[r + 1, t] + cs[x, :, cols] * south)
                    + (cn[x, :, cols] * north + drive)
                )
                target[GUARD + x, :, cols] = fresh
                now[x, :, cols] = twice[x, :, cols] * later[x, :, cols] - drive
                if keep and t < tiles - 1:
                    snap[x - REACH, pl.ds(pl.multiple_of(step * subs, subs), subs), cols] = fresh

    def copy_out(step):
        part = pl.ds(pl.multiple_of(step * subs, subs), subs)
        return pltpu.make_async_copy(snap.at[:, part, :], snap_ref.at[:, part, :], sems.at[step])

    def one(source, target, now, later, step):
        low = (step + 1) // BATCH
        high = (total - 1 - step + BATCH - 1) // BATCH

        def halo_rows(i, carry):
            advance(source, target, now, later, i * BATCH, BATCH, step, False)
            return carry

        def own_rows(i, carry):
            advance(source, target, now, later, REACH + i * OWN, OWN, step, True)
            return carry

        def drift_rows(i, carry):
            part = pl.ds(i * BATCH, BATCH)
            now[part] = twice[part] * later[part] - now[part]
            return carry

        lax.fori_loop(0, rows // OWN, own_rows, 0)
        copy_out(step).start()
        lax.fori_loop(low, REACH // BATCH, halo_rows, 0)
        lax.fori_loop((REACH + rows) // BATCH, high, halo_rows, 0)
        if keep_drift:
            lax.fori_loop(0, low, drift_rows, 0)
            lax.fori_loop(high, total // BATCH, drift_rows, 0)

    def pair(i, carry):
        one(qa, qb, xa, xb, 2 * i)
        one(qb, qa, xb, xa, 2 * i + 1)
        return carry

    lax.fori_loop(0, REACH // 2, pair, 0)

    def drain():
        def drained(step, carry):
            copy_out(step).wait()
            return carry

        lax.fori_loop(0, REACH, drained, 0)

    return drain


def first_kernel(groups, halves, *refs):
    sources = [refs[3 * i : 3 * i + 3] for i in range(groups)]
    snap_ref, carry_ref, low_ref, own_ref, high_ref = refs[3 * groups : 3 * groups + 5]
    refs = refs[3 * groups + 5 :]
    grid, (snap, sems, carry_sems) = refs[:10], refs[10:]
    qa, qb, xa, xb, twice, cw, ce, cs, cn, c0 = grid
    rows = sources[0][1].shape[1]
    block = sources[0][1].shape[2] - TILE
    length = block // halves
    tiles = length // TILE + 1
    subs = halves * groups * 2
    me = lax.axis_index("tm")
    offsets = (0, REACH, REACH + rows)

    sub = lax.broadcasted_iota(jnp.int32, (1, subs, TILE), 1)
    kappa = jnp.where((sub & 1) == 0, np.float32(KAPPA[0]), np.float32(KAPPA[1]))
    half_of = sub // (2 * groups)
    lane3 = lanes_of((1, subs, TILE))
    lowest = (me == 0) & (half_of == 0) & (lane3 >= TILE // 2)
    highest = (me == groups - 1) & (half_of == halves - 1) & (lane3 < TILE // 2)
    inside = jnp.where(lowest | highest, 0.0, 1.0).astype(jnp.float32)
    lane2 = lanes_of((8, TILE))

    def turned(parts):
        return jnp.swapaxes(jnp.stack(parts, axis=0), 0, 1)

    def prepare(place, base, tile, halo):
        def cut(ref, index, half):
            line = pl.ds(base, 8)
            if not halo:
                return ref[index, line, pl.ds(pl.multiple_of(half * length + tile * TILE, TILE), TILE)]
            above = (half + 1) * length
            below = half * length - TILE if half > 0 else block
            high = ref[index, line, above : above + TILE]
            if above == below:
                return high
            low = ref[index, line, below : below + TILE]
            return jnp.where(lane2 < TILE // 2, high, low)

        own = sources[0][place]
        starts, first, second, flow_x, flow_y, doubled = [], [], [], [], [], []
        for half in range(halves):
            vx, vy, amp, freq, phase = (cut(own, index, half) for index in range(5))
            sin_f, cos_f = sin_cos(freq)
            for group in range(groups):
                ref, at = sources[group][place], 5 if group == 0 else 0
                step = ref[at, pl.ds(base, 8), block : block + TILE][:, TILE // 2 : TILE // 2 + 1]
                s, c = sin_cos(freq * step + phase)
                s, c = amp * s, amp * c
                for field in range(2):
                    starts.append(cut(ref, at + field, half))
                    x, y = (s, c) if field == 0 else (0.5 * c, -0.5 * s)
                    first.append(x)
                    second.append(x * cos_f + y * sin_f)
                    flow_x.append(vx)
                    flow_y.append(vy)
                    doubled.append(2.0 * cos_f)
        where = pl.ds(offsets[place] + base, 8)
        columns = pl.ds(pl.multiple_of(tile * TILE, TILE), TILE)
        vx, vy = turned(flow_x), turned(flow_y)
        west = kappa + jnp.maximum(vx, 0.0)
        east = kappa - jnp.minimum(vx, 0.0)
        south = kappa + jnp.maximum(vy, 0.0)
        north = kappa - jnp.minimum(vy, 0.0)
        centre = 1.0 - (west + east + south + north)
        state, x0, x1 = turned(starts), turned(first), turned(second)
        if halo:
            west, east, south, north, centre, state, x0, x1 = (
                v * inside for v in (west, east, south, north, centre, state, x0, x1)
            )
        cw[where, :, columns] = west
        ce[where, :, columns] = east
        cs[where, :, columns] = south
        cn[where, :, columns] = north
        c0[where, :, columns] = centre
        xa[where, :, columns] = x0
        xb[where, :, columns] = x1
        twice[where, :, columns] = turned(doubled)
        qa[pl.ds(GUARD + offsets[place] + base, 8), :, columns] = state

    for place, count in ((0, REACH), (1, rows), (2, REACH)):

        def by_rows(number, carry, place=place):
            base = pl.multiple_of(number * 8, 8)

            def by_tiles(tile, inner):
                prepare(place, base, tile, False)
                return inner

            lax.fori_loop(0, tiles - 1, by_tiles, 0)
            prepare(place, base, tiles - 1, True)
            return carry

        lax.fori_loop(0, count // 8, by_rows, 0)

    def keep(i):
        return pltpu.make_async_copy(grid[2 + i], carry_ref.at[i], carry_sems.at[i])

    for i in range(2, 8):
        keep(i).start()
    drain = run_phase(grid, rows, snap, snap_ref, sems, True)
    for i in range(2):
        keep(i).start()
    low_ref[...] = qa[GUARD + REACH : GUARD + 2 * REACH]
    own_ref[...] = qa[GUARD + REACH : GUARD + REACH + rows]
    high_ref[...] = qa[GUARD + rows : GUARD + rows + REACH]
    drain()
    for i in range(8):
        keep(i).wait()


def split_rows(a):
    high = a.astype(jnp.bfloat16)
    return jnp.concatenate([high, (a - high.astype(jnp.float32)).astype(jnp.bfloat16)], axis=0)


def outer_of(a, b):
    return lax.dot_general(a, b, (((1,), (1,)), ((), ())), preferred_element_type=jnp.float32)


def joined(g):
    m, n = g.shape[0] // 2, g.shape[1] // 2
    return (g[:m, :n] + g[m:, n:]) + (g[:m, n:] + g[m:, :n])


def gram_kernel(snap_ref, gram_ref):
    width = snap_ref.shape[1]

    @pl.when(pl.program_id(0) == 0)
    def _():
        gram_ref[...] = jnp.zeros_like(gram_ref)

    total = jnp.zeros((2 * width, 2 * width), jnp.float32)
    for x in range(snap_ref.shape[0]):
        both = split_rows(snap_ref[x])
        total = total + outer_of(both, both)
    gram_ref[...] += joined(total)


def second_kernel(groups, halves, with_left, left_halo, own, right_halo, carry_ref, earlier_ref, *refs):
    if with_left:
        gram_ref, select_ref, fold_ref = refs[:3]
        refs = refs[3:]
        snap_ref, end_ref, left_ref = refs[:3]
        refs = refs[3:]
    else:
        snap_ref, end_ref = refs[:2]
        refs = refs[2:]
    grid, (snap, earlier, sems, carry_sems, more_sems) = refs[:10], refs[10:]
    qa = grid[0]
    rows, width, length = snap.shape
    subs = qa.shape[1]
    tiles = length // TILE + 1

    def bring(i):
        return pltpu.make_async_copy(carry_ref.at[i], grid[2 + i], carry_sems.at[i])

    late = pltpu.make_async_copy(earlier_ref, earlier, more_sems.at[0])
    for i in range(8):
        bring(i).start()
    if with_left:
        late.start()
    qa[GUARD : GUARD + REACH] = left_halo[...]
    qa[GUARD + REACH : GUARD + REACH + rows] = own[...]
    qa[GUARD + REACH + rows : GUARD + 2 * REACH + rows] = right_halo[...]
    for i in range(8):
        bring(i).wait()
    drain = run_phase(grid, rows, snap, snap_ref, sems, False)

    for base in range(0, rows, 8):
        for t in range(tiles - 1):
            cols = slice(t * TILE, (t + 1) * TILE)
            value = jnp.swapaxes(qa[GUARD + REACH + base : GUARD + REACH + base + 8, :, cols], 0, 1)
            for half in range(halves):
                for group in range(groups):
                    for field in range(2):
                        end_ref[
                            group, field, base : base + 8, half * length + t * TILE : half * length + (t + 1) * TILE
                        ] = value[half * groups * 2 + group * 2 + field]

    if with_left:
        late.wait()

        def add(x, total):
            now = split_rows(snap[x])
            every = jnp.concatenate([now, split_rows(earlier[x])], axis=0)
            return total + outer_of(now, every)

        both = lax.fori_loop(0, rows, add, jnp.zeros((2 * width, 4 * width), jnp.float32))
        late_late, late_early = joined(both[:, : 2 * width]), joined(both[:, 2 * width :])
        lane = lanes_of((1, width))
        result = jnp.zeros(left_ref.shape, jnp.float32)
        for half in range(halves):
            inside = (lane % subs) // (2 * groups) == half
            at = half * 2 * width
            early, later = select_ref[:, at : at + width], select_ref[:, at + width : at + 2 * width]
            part = mm(early, gram_ref[...]) + mm(later, late_early)
            result = result + mm(jnp.where(inside, part, 0.0), fold_ref[:width])
            part = mm_nt(early, late_early) + mm(later, late_late)
            result = result + mm(jnp.where(inside, part, 0.0), fold_ref[width:])
        left_ref[...] = result
    drain()


def eliminate(m, rank):
    row = lax.broadcasted_iota(jnp.int32, m.shape, 0)
    lane = lanes_of(m.shape)
    for k in range(0, rank, 2):
        line, after = m[k : k + 1, :], m[k + 1 : k + 2, :]
        column = jnp.broadcast_to(m[:, k : k + 1], m.shape)
        beside = jnp.broadcast_to(m[:, k + 1 : k + 2], m.shape)
        a, b, d = column[k : k + 1], column[k + 1 : k + 2], beside[k + 1 : k + 2]
        inverse = 1.0 / a
        ratio = b * inverse
        pivot = 1.0 / (d - ratio * b)
        after = after - ratio * line
        beside = (beside - ratio * column) * pivot
        m = (
            m
            - jnp.where(row > k, column * inverse, 0.0) * line
            - jnp.where(row > k + 1, beside, 0.0) * after
        )
    diagonal = jnp.sum(jnp.where(row == lane, m, 0.0), axis=1, keepdims=True)
    return m * lax.rsqrt(diagonal)


def in_two(x):
    high = x.astype(jnp.bfloat16)
    return high, (x - high.astype(jnp.float32)).astype(jnp.bfloat16)


CHUNK = 256


def merge_kernel(halves, left_ref, spread_ref, unit_ref, expand_ref, early_ref, late_ref, out_ref, snap, out, arrived, left_sems):
    rank = left_ref.shape[0]
    wide = left_ref.shape[1]
    rows, width, length = snap.shape
    parts = length // CHUNK

    def fetch(i, part):
        at = pl.ds(i * CHUNK, CHUNK)
        ref = (early_ref, late_ref)[part]
        columns = pl.ds(part * (width // 2), width // 2)
        return pltpu.make_async_copy(ref.at[:, :, at], snap.at[:, columns, at], arrived.at[i, part])

    def store(i, half):
        at = pl.ds(half * length + i * CHUNK, CHUNK)
        return pltpu.make_async_copy(out.at[:, :, at], out_ref.at[:, :, at], left_sems.at[i, half])

    for i in range(parts):
        fetch(i, 0).start()
        fetch(i, 1).start()
    lane = lanes_of((rank, 128))
    whole = eliminate(mm(left_ref[...], spread_ref[...]) + unit_ref[...], rank)
    proj = jnp.where((lane >= rank) & (lane < rank + wide), whole, 0.0)
    outer = mm_nt(proj, proj)
    factor = eliminate(outer, rank)
    upper = jnp.where(
        lax.broadcasted_iota(jnp.int32, (rank, rank), 0) <= lanes_of((rank, rank)), factor, 0.0
    )
    mix = mm(upper, whole)
    weights = jnp.concatenate(
        [mm(mix, expand_ref[:, half * width : (half + 1) * width]) for half in range(halves)], axis=0
    )
    count = halves * rank
    high, low = in_two(weights)
    weights = jnp.concatenate(
        [jnp.concatenate([high, high], axis=1), jnp.concatenate([low, low], axis=1)], axis=0
    )
    for i in range(parts):
        fetch(i, 0).wait()
        fetch(i, 1).wait()
        for base in range(0, rows, 8):
            made = []
            for x in range(base, base + 8):
                values = jnp.concatenate(in_two(snap[x, :, i * CHUNK : (i + 1) * CHUNK]), axis=0)
                both = jnp.dot(weights, values, preferred_element_type=jnp.float32)
                made.append(both[:count] + both[count:])
            for half in range(halves):
                at = half * length + i * CHUNK
                for r in range(0, rank, 8):
                    first = half * rank + r
                    block = jnp.stack([p[first : first + 8] for p in made], axis=0)
                    out[r : r + 8, base : base + 8, at : at + CHUNK] = jnp.swapaxes(block, 0, 1)
        for half in range(halves):
            store(i, half).start()
    for i in range(parts):
        for half in range(halves):
            store(i, half).wait()


def shifted(value, along_space, along_tm):
    space, tm = lax.axis_size("space"), lax.axis_size("tm")
    moves = [
        (s * tm + t, (s + along_space) % space * tm + (t + along_tm) % tm)
        for s in range(space)
        for t in range(tm)
    ]
    return lax.ppermute(value, AXES, moves)


def turn(value, start):
    return lax.dynamic_slice_in_dim(jnp.concatenate([value, value]), start, value.shape[0], 0)


def total_of(value):
    size = lax.axis_size("space") * lax.axis_size("tm")
    if size & (size - 1):
        return lax.psum(value, AXES)
    bit = 1
    while bit < size:
        value = value + lax.ppermute(value, AXES, [(i, i ^ bit) for i in range(size)])
        bit *= 2
    return value


def coefficients(gram, sketch):
    left = jnp.dot(sketch.T, gram, precision=HIGHEST)
    small = jnp.dot(left, sketch, precision=HIGHEST)
    lower = jnp.linalg.cholesky(small)
    proj = lax.linalg.triangular_solve(lower, left, left_side=True, lower=True)
    outer = jnp.dot(proj, proj.T, precision=HIGHEST)
    factor = jnp.linalg.cholesky(outer)
    mix = lax.linalg.triangular_solve(lower, factor, left_side=True, lower=True, transpose_a=True)
    return jnp.dot(sketch, mix, precision=HIGHEST)


def merge_levels(pieces, sketch):
    while pieces.shape[0] > 1:
        count, columns, rows, length = pieces.shape
        joined = pieces.reshape(count // 2, 2 * columns, rows, length)
        gram = jnp.einsum("gcxy,gdxy->gcd", joined, joined, precision=HIGHEST)
        gram = lax.psum(gram, AXES)
        coeff = jax.vmap(coefficients, in_axes=(0, None))(gram, sketch)
        pieces = jnp.einsum("gcxy,gcr->grxy", joined, coeff, precision=HIGHEST)
    return pieces[0]


def body(start_state, start_step, velocity_x, velocity_y, amplitude, frequency, phase, sketch):
    groups = lax.axis_size("tm")
    me = lax.axis_index("tm")
    rows, full = velocity_x.shape
    block = full // groups
    halves = max(1, 8 // (2 * groups))
    subs = halves * groups * 2
    length = block // halves
    span = length + TILE
    width = STEPS * subs
    fast = groups == 2
    f32 = jnp.float32

    total = rows + 2 * REACH
    shapes = [jax.ShapeDtypeStruct((7, count, block + TILE), f32) for count in (REACH, rows, REACH)]
    for _ in range(groups - 1):
        shapes += [jax.ShapeDtypeStruct((2, count, block + TILE), f32) for count in (REACH, rows, REACH)]
    packed = pl.pallas_call(
        functools.partial(pack_kernel, groups, block),
        out_shape=shapes,
        in_specs=[SMEM] + [VMEM] * 6,
        out_specs=[VMEM] * len(shapes),
        name="pack",
    )(start_step, start_state, velocity_x, velocity_y, amplitude, frequency, phase)
    sources = [shifted(packed[2], 1, 0), packed[1], shifted(packed[0], -1, 0)]
    for shift in range(1, groups):
        low, every, high = packed[3 * shift : 3 * shift + 3]
        sources += [shifted(high, 1, shift), shifted(every, 0, shift), shifted(low, -1, shift)]

    extra = []
    if fast:
        column = np.arange(width)
        half_of = column % subs // (2 * groups)
        picks = np.zeros((groups, halves, 2 * STEPS * groups, width), np.float32)
        for member in range(groups):
            group = (member - column % (2 * groups) // 2) % groups
            index = group * 2 * STEPS + column % 2 * STEPS + column // subs
            picks[member, half_of, index, column] = 1.0
        pick = lax.dynamic_index_in_dim(jnp.asarray(picks), me, 0, keepdims=False)
        pick = jnp.concatenate([pick[half] for half in range(halves)], axis=1)
        select = jnp.dot(sketch.T, pick, precision=HIGHEST)
        fold = sum(pick[:, half * width : (half + 1) * width] for half in range(halves)).T
        rank, wide = sketch.shape[1], sketch.shape[0]
        spread = jnp.concatenate(
            [sketch, jnp.eye(wide, dtype=f32), jnp.zeros((wide, 128 - rank - wide), f32)], axis=1
        )
        unit = jnp.eye(rank, 128, 128 - rank, dtype=f32)
        expand = jnp.concatenate([jnp.zeros((128 - rank, halves * width), f32), select], axis=0)
        extra = [select, fold]

    grid = [pltpu.VMEM((total + 2 * GUARD, subs, span), f32)] * 2 + [pltpu.VMEM((total, subs, span), f32)] * 8
    half_snap = (rows, width // 2, length)
    early, carry, low, own, high = pl.pallas_call(
        functools.partial(first_kernel, groups, halves),
        out_shape=[
            pltpu.HBM(half_snap, f32),
            pltpu.HBM((8, total, subs, span), f32),
            jax.ShapeDtypeStruct((REACH, subs, span), f32),
            jax.ShapeDtypeStruct((rows, subs, span), f32),
            jax.ShapeDtypeStruct((REACH, subs, span), f32),
        ],
        in_specs=[VMEM] * len(sources),
        out_specs=[HBM] * 2 + [VMEM] * 3,
        scratch_shapes=grid
        + [pltpu.VMEM(half_snap, f32), pltpu.SemaphoreType.DMA((REACH,)), pltpu.SemaphoreType.DMA((8,))],
        compiler_params=pltpu.CompilerParams(vmem_limit_bytes=36 * 2**20),
        name="first",
    )(*sources)
    beside = [shifted(high, 1, 0), own, shifted(low, -1, 0)]
    outs = [pltpu.HBM(half_snap, f32), jax.ShapeDtypeStruct((groups, 2, rows, block), f32)]
    if fast:
        outs.append(jax.ShapeDtypeStruct((sketch.shape[1], sketch.shape[0]), f32))
        gram = pl.pallas_call(
            gram_kernel,
            out_shape=jax.ShapeDtypeStruct((width // 2, width // 2), f32),
            grid=(4,),
            in_specs=[pl.BlockSpec((rows // 4, width // 2, length), lambda i: (i, 0, 0))],
            out_specs=pl.BlockSpec((width // 2, width // 2), lambda i: (0, 0)),
            cost_estimate=pl.CostEstimate(flops=2 * rows * width * width * length, bytes_accessed=2 * rows * width * length, transcendentals=0),
            compiler_params=pltpu.CompilerParams(vmem_limit_bytes=16 * 2**20),
            name="gram",
        )(early)
        extra = [gram] + extra
    made = pl.pallas_call(
        functools.partial(second_kernel, groups, halves, fast),
        out_shape=outs,
        in_specs=[VMEM] * 3 + [HBM] * 2 + [VMEM] * len(extra),
        out_specs=[HBM] + [VMEM] * (len(outs) - 1),
        scratch_shapes=grid
        + [pltpu.VMEM(half_snap, f32)] * 2
        + [pltpu.SemaphoreType.DMA((REACH,)), pltpu.SemaphoreType.DMA((8,)), pltpu.SemaphoreType.DMA((1,))],
        compiler_params=pltpu.CompilerParams(vmem_limit_bytes=40 * 2**20),
        name="second",
    )(*beside, carry, early, *extra)

    if fast:
        left = total_of(made[2])
        piece = pl.pallas_call(
            functools.partial(merge_kernel, halves),
            out_shape=jax.ShapeDtypeStruct((rank, rows, block), f32),
            in_specs=[VMEM] * 4 + [HBM] * 2,
            out_specs=HBM,
            scratch_shapes=[
                pltpu.VMEM((rows, width, length), f32),
                pltpu.VMEM((rank, rows, block), f32),
                pltpu.SemaphoreType.DMA((length // CHUNK, 2)),
                pltpu.SemaphoreType.DMA((length // CHUNK, halves)),
            ],
            compiler_params=pltpu.CompilerParams(vmem_limit_bytes=54 * 2**20),
            name="merge",
        )(left, spread, unit, expand, early, made[0])
    else:
        snaps = jnp.concatenate([early, made[0]], axis=1).reshape(rows, STEPS, halves, groups, 2, length)
        snaps = jnp.transpose(snaps, (3, 4, 1, 0, 2, 5)).reshape(groups, 2 * STEPS, rows, block)
        snaps = turn(jnp.flip(snaps, 0), groups - 1 - me)
        piece = merge_levels(snaps, sketch)

    ends = [made[1][0]]
    for shift in range(1, groups):
        ends.append(shifted(made[1][shift], 0, groups - shift))
    if groups == 2:
        end_state = jnp.where(
            me == 0,
            jnp.concatenate([ends[0], ends[1]], axis=-1),
            jnp.concatenate([ends[1], ends[0]], axis=-1),
        )
    else:
        stacked = turn(jnp.stack(ends), groups - me)
        end_state = jnp.moveaxis(stacked, 0, -2).reshape(2, rows, full)
    return (piece, end_state[None])


def solution(mesh):
    placed = (
        P("tm", None, "space", None),
        P("tm"),
        P("space", None),
        P("space", None),
        P("space", None),
        P("space", None),
        P("space", None),
        P(),
    )
    return jax.shard_map(
        body,
        mesh=mesh,
        in_specs=placed,
        out_specs=(P(None, "space", "tm"), P("tm", None, "space", None)),
        check_vma=False,
    )
```

```python
import functools

import jax
import jax.numpy as jnp
import numpy as np
from jax import lax
from jax.experimental import pallas as pl
from jax.experimental.pallas import tpu as pltpu
from jax.sharding import PartitionSpec as P

STEPS = 16
KAPPA = (0.06, 0.02)
HIGHEST = lax.Precision.HIGHEST
AXES = ("space", "tm")
TILE = 128
GUARD = 8
BATCH = 4
OWN = 8
REACH = STEPS // 2
VMEM = pl.BlockSpec(memory_space=pltpu.VMEM)
ANY = pl.BlockSpec(memory_space=pl.ANY)
HBM = pl.BlockSpec(memory_space=pltpu.HBM)
SMEM = pl.BlockSpec(memory_space=pltpu.SMEM)


def mm(a, b):
    return jnp.dot(a, b, precision=HIGHEST, preferred_element_type=jnp.float32)


def mm_nt(a, b):
    return lax.dot_general(
        a, b, (((1,), (1,)), ((), ())), precision=HIGHEST, preferred_element_type=jnp.float32
    )


def lanes_of(shape):
    return lax.broadcasted_iota(jnp.int32, shape, len(shape) - 1)


def pack_kernel(groups, block, step_ref, *refs):
    out_refs, scratch, sems = refs[6:-7], refs[-7:-1], refs[-1]
    brought = [pltpu.make_async_copy(refs[i], scratch[i], sems.at[i]) for i in range(6)]
    for copy in brought:
        copy.start()
    state_ref, vx, vy, amp, freq, phase = scratch
    full = vx.shape[1]
    me = lax.axis_index("tm")
    start = step_ref[0].astype(jnp.float32)
    rows = vx.shape[0]
    lane = lanes_of((rows, TILE))

    def cut(read, target, write, is_state):
        first = target * block
        write(pl.ds(0, block), read(pl.ds(pl.multiple_of(first, TILE), block)))
        above = jnp.minimum(first + block, full - TILE)
        below = jnp.maximum(first - TILE, 0)
        high = read(pl.ds(pl.multiple_of(above, TILE), TILE))
        low = read(pl.ds(pl.multiple_of(below, TILE), TILE))
        high = jnp.where(target < groups - 1, high, 0.0)
        low = jnp.where(target > 0, low, 0.0)
        halo = jnp.where(lane < TILE // 2, high, low)
        if is_state:
            halo = jnp.where((lane >= TILE // 4) & (lane < 3 * TILE // 4), start, halo)
        write(pl.ds(block, TILE), halo)

    def writer(group, index):
        low, every, high = out_refs[3 * group : 3 * group + 3]

        def write(columns, value):
            low[index, :, columns] = value[:REACH]
            every[index, :, columns] = value
            high[index, :, columns] = value[rows - REACH :]

        return write

    for index, ref in enumerate((vx, vy, amp, freq, phase)):
        brought[1 + index].wait()
        cut(lambda columns, ref=ref: ref[:, columns], me, writer(0, index), False)
    brought[0].wait()
    for shift in range(groups):
        target = lax.rem(me + shift, groups)
        for field in range(2):
            write = writer(shift, 5 + field if shift == 0 else field)
            cut(lambda columns, field=field: state_ref[0, field, :, columns], target, write, True)


def sin_cos(angle):
    turns = jnp.floor(angle * np.float32(2.0 / np.pi) + 0.5)
    r = angle - turns * np.float32(1.5703125)
    r = r - turns * np.float32(4.837512969970703125e-4)
    r = r - turns * np.float32(7.54978995489188216e-8)
    z = r * r
    sine = r + r * z * (
        np.float32(-1.6666654611e-1)
        + z * (np.float32(8.3321608736e-3) + z * np.float32(-1.9515295891e-4))
    )
    cosine = (
        1.0
        - 0.5 * z
        + z
        * z
        * (
            np.float32(4.166664568298827e-2)
            + z * (np.float32(-1.388731625493765e-3) + z * np.float32(2.443315711809948e-5))
        )
    )
    quadrant = turns.astype(jnp.int32)
    odd = (quadrant & 1) == 1
    s = jnp.where(odd, cosine, sine)
    c = jnp.where(odd, sine, cosine)
    s = jnp.where((quadrant & 2) == 2, -s, s)
    c = jnp.where(((quadrant + 1) & 2) == 2, -c, c)
    return s, c


def run_phase(grid, rows, snap, snap_ref, sems, keep_drift):
    qa, qb, xa, xb, twice, cw, ce, cs, cn, c0 = grid
    subs = qa.shape[1]
    tiles = qa.shape[2] // TILE
    total = rows + 2 * REACH

    for guard in (GUARD - 1, GUARD + total):
        qa[guard] = jnp.zeros(qa.shape[1:], jnp.float32)
        qb[guard] = jnp.zeros(qb.shape[1:], jnp.float32)

    lane2s = lanes_of((subs, TILE))
    first_lane, last_lane = lane2s == 0, lane2s == TILE - 1

    def advance(source, target, now, later, row, count, step, keep):
        def tile_of(r, t):
            return source[GUARD + row + r, :, t * TILE : (t + 1) * TILE]

        held, up, down = {}, {}, {}

        def load(t):
            for r in range(-1, count + 1):
                held[r, t] = tile_of(r, t)
            for r in range(count):
                up[r, t] = pltpu.roll(held[r, t], 1, 1)
                down[r, t] = pltpu.roll(held[r, t], TILE - 1, 1)

        load(tiles - 1)
        load(0)
        for r in range(count):
            up[r, -1], down[r, tiles] = up[r, tiles - 1], down[r, 0]
        for t in range(tiles):
            if t + 1 < tiles - 1:
                load(t + 1)
            cols = slice(t * TILE, (t + 1) * TILE)
            for r in range(count):
                x = row + r
                south = jnp.where(first_lane, up[r, t - 1], up[r, t])
                north = jnp.where(last_lane, down[r, t + 1], down[r, t])
                drive = now[x, :, cols]
                fresh = (
                    (c0[x, :, cols] * held[r, t] + cw[x, :, cols] * held[r - 1, t])
                    + (ce[x, :, cols] * held[r + 1, t] + cs[x, :, cols] * south)
                    + (cn[x, :, cols] * north + drive)
                )
                target[GUARD + x, :, cols] = fresh
                now[x, :, cols] = twice[x, :, cols] * later[x, :, cols] - drive
                if keep and t < tiles - 1:
                    snap[x - REACH, pl.ds(pl.multiple_of(step * subs, subs), subs), cols] = fresh

    def copy_out(step):
        part = pl.ds(pl.multiple_of(step * subs, subs), subs)
        return pltpu.make_async_copy(snap.at[:, part, :], snap_ref.at[:, part, :], sems.at[step])

    def one(source, target, now, later, step):
        low = (step + 1) // BATCH
        high = (total - 1 - step + BATCH - 1) // BATCH

        def halo_rows(i, carry):
            advance(source, target, now, later, i * BATCH, BATCH, step, False)
            return carry

        def own_rows(i, carry):
            advance(source, target, now, later, REACH + i * OWN, OWN, step, True)
            return carry

        def drift_rows(i, carry):
            part = pl.ds(i * BATCH, BATCH)
            now[part] = twice[part] * later[part] - now[part]
            return carry

        lax.fori_loop(0, rows // OWN, own_rows, 0)
        copy_out(step).start()
        lax.fori_loop(low, REACH // BATCH, halo_rows, 0)
        lax.fori_loop((REACH + rows) // BATCH, high, halo_rows, 0)
        if keep_drift:
            lax.fori_loop(0, low, drift_rows, 0)
            lax.fori_loop(high, total // BATCH, drift_rows, 0)

    def pair(i, carry):
        one(qa, qb, xa, xb, 2 * i)
        one(qb, qa, xb, xa, 2 * i + 1)
        return carry

    lax.fori_loop(0, REACH // 2, pair, 0)

    def drain():
        def drained(step, carry):
            copy_out(step).wait()
            return carry

        lax.fori_loop(0, REACH, drained, 0)

    return drain


def first_kernel(groups, halves, *refs):
    sources = [refs[3 * i : 3 * i + 3] for i in range(groups)]
    snap_ref, carry_ref, low_ref, own_ref, high_ref = refs[3 * groups : 3 * groups + 5]
    refs = refs[3 * groups + 5 :]
    qa, qb, snap, sems = refs
    xa, xb, twice, cw, ce, cs, cn, c0 = (carry_ref.at[i] for i in range(8))
    grid = (qa, qb, xa, xb, twice, cw, ce, cs, cn, c0)
    rows = sources[0][1].shape[1]
    block = sources[0][1].shape[2] - TILE
    length = block // halves
    tiles = length // TILE + 1
    subs = halves * groups * 2
    me = lax.axis_index("tm")
    offsets = (0, REACH, REACH + rows)

    sub = lax.broadcasted_iota(jnp.int32, (1, subs, TILE), 1)
    kappa = jnp.where((sub & 1) == 0, np.float32(KAPPA[0]), np.float32(KAPPA[1]))
    half_of = sub // (2 * groups)
    lane3 = lanes_of((1, subs, TILE))
    lowest = (me == 0) & (half_of == 0) & (lane3 >= TILE // 2)
    highest = (me == groups - 1) & (half_of == halves - 1) & (lane3 < TILE // 2)
    inside = jnp.where(lowest | highest, 0.0, 1.0).astype(jnp.float32)
    lane2 = lanes_of((8, TILE))

    def turned(parts):
        return jnp.swapaxes(jnp.stack(parts, axis=0), 0, 1)

    def prepare(place, base, tile, halo):
        def cut(ref, index, half):
            line = pl.ds(base, 8)
            if not halo:
                return ref[index, line, pl.ds(pl.multiple_of(half * length + tile * TILE, TILE), TILE)]
            above = (half + 1) * length
            below = half * length - TILE if half > 0 else block
            high = ref[index, line, above : above + TILE]
            if above == below:
                return high
            low = ref[index, line, below : below + TILE]
            return jnp.where(lane2 < TILE // 2, high, low)

        own = sources[0][place]
        starts, first, second, flow_x, flow_y, doubled = [], [], [], [], [], []
        for half in range(halves):
            vx, vy, amp, freq, phase = (cut(own, index, half) for index in range(5))
            sin_f, cos_f = sin_cos(freq)
            for group in range(groups):
                ref, at = sources[group][place], 5 if group == 0 else 0
                step = ref[at, pl.ds(base, 8), block : block + TILE][:, TILE // 2 : TILE // 2 + 1]
                s, c = sin_cos(freq * step + phase)
                s, c = amp * s, amp * c
                for field in range(2):
                    starts.append(cut(ref, at + field, half))
                    x, y = (s, c) if field == 0 else (0.5 * c, -0.5 * s)
                    first.append(x)
                    second.append(x * cos_f + y * sin_f)
                    flow_x.append(vx)
                    flow_y.append(vy)
                    doubled.append(2.0 * cos_f)
        where = pl.ds(offsets[place] + base, 8)
        columns = pl.ds(pl.multiple_of(tile * TILE, TILE), TILE)
        vx, vy = turned(flow_x), turned(flow_y)
        west = kappa + jnp.maximum(vx, 0.0)
        east = kappa - jnp.minimum(vx, 0.0)
        south = kappa + jnp.maximum(vy, 0.0)
        north = kappa - jnp.minimum(vy, 0.0)
        centre = 1.0 - (west + east + south + north)
        state, x0, x1 = turned(starts), turned(first), turned(second)
        if halo:
            west, east, south, north, centre, state, x0, x1 = (
                v * inside for v in (west, east, south, north, centre, state, x0, x1)
            )
        cw[where, :, columns] = west
        ce[where, :, columns] = east
        cs[where, :, columns] = south
        cn[where, :, columns] = north
        c0[where, :, columns] = centre
        xa[where, :, columns] = x0
        xb[where, :, columns] = x1
        twice[where, :, columns] = turned(doubled)
        qa[pl.ds(GUARD + offsets[place] + base, 8), :, columns] = state

    for place, count in ((0, REACH), (1, rows), (2, REACH)):

        def by_rows(number, carry, place=place):
            base = pl.multiple_of(number * 8, 8)

            def by_tiles(tile, inner):
                prepare(place, base, tile, False)
                return inner

            lax.fori_loop(0, tiles - 1, by_tiles, 0)
            prepare(place, base, tiles - 1, True)
            return carry

        lax.fori_loop(0, count // 8, by_rows, 0)

    drain = run_phase(grid, rows, snap, snap_ref, sems, True)
    low_ref[...] = qa[GUARD + REACH : GUARD + 2 * REACH]
    own_ref[...] = qa[GUARD + REACH : GUARD + REACH + rows]
    high_ref[...] = qa[GUARD + rows : GUARD + rows + REACH]
    drain()


def split_rows(a):
    high = a.astype(jnp.bfloat16)
    return jnp.concatenate([high, (a - high.astype(jnp.float32)).astype(jnp.bfloat16)], axis=0)


def outer_of(a, b):
    return lax.dot_general(a, b, (((1,), (1,)), ((), ())), preferred_element_type=jnp.float32)


def joined(g):
    m, n = g.shape[0] // 2, g.shape[1] // 2
    return (g[:m, :n] + g[m:, n:]) + (g[:m, n:] + g[m:, :n])


def gram_kernel(snap_ref, gram_ref, snap, sems):
    rows, width, _ = snap.shape
    parts = sems.shape[0]
    depth = rows // parts

    def fetch(i):
        at = pl.ds(i * depth, depth)
        return pltpu.make_async_copy(snap_ref.at[at], snap.at[at], sems.at[i])

    for i in range(parts):
        fetch(i).start()
    total = jnp.zeros((2 * width, 2 * width), jnp.float32)
    for i in range(parts):
        fetch(i).wait()
        for x in range(i * depth, (i + 1) * depth):
            both = split_rows(snap[x])
            total = total + outer_of(both, both)
    gram_ref[...] = joined(total)


def second_kernel(groups, halves, with_left, left_halo, own, right_halo, carry_ref, earlier, *refs):
    if with_left:
        gram_ref, select_ref, fold_ref = refs[:3]
        refs = refs[3:]
        snap_ref, kept_ref, sent_ref, left_ref = refs[:4]
        refs = refs[4:]
    else:
        snap_ref, kept_ref, sent_ref = refs[:3]
        refs = refs[3:]
    qa, qb, xa, xb, snap, sems = refs
    grid = [qa, qb, xa, xb] + [carry_ref.at[i] for i in range(2, 8)]
    rows, width, length = snap.shape
    subs = qa.shape[1]
    tiles = length // TILE + 1

    xa[...] = carry_ref[0]
    xb[...] = carry_ref[1]
    qa[GUARD : GUARD + REACH] = left_halo[...]
    qa[GUARD + REACH : GUARD + REACH + rows] = own[...]
    qa[GUARD + REACH + rows : GUARD + 2 * REACH + rows] = right_halo[...]
    drain = run_phase(grid, rows, snap, snap_ref, sems, False)

    for base in range(0, rows, 8):
        for t in range(tiles - 1):
            cols = slice(t * TILE, (t + 1) * TILE)
            value = jnp.swapaxes(qa[GUARD + REACH + base : GUARD + REACH + base + 8, :, cols], 0, 1)
            for half in range(halves):
                for group in range(groups):
                    for field in range(2):
                        end_ref = kept_ref if group == 0 else sent_ref.at[group - 1]
                        end_ref[field, base : base + 8, half * length + t * TILE : half * length + (t + 1) * TILE] = value[half * groups * 2 + group * 2 + field]

    if with_left:
        def add(x, total):
            now = split_rows(snap[x])
            every = jnp.concatenate([now, split_rows(earlier[x])], axis=0)
            return total + outer_of(now, every)

        both = lax.fori_loop(0, rows, add, jnp.zeros((2 * width, 4 * width), jnp.float32))
        late_late, late_early = joined(both[:, : 2 * width]), joined(both[:, 2 * width :])
        lane = lanes_of((1, width))
        result = jnp.zeros(left_ref.shape, jnp.float32)
        for half in range(halves):
            inside = (lane % subs) // (2 * groups) == half
            at = half * 2 * width
            early, later = select_ref[:, at : at + width], select_ref[:, at + width : at + 2 * width]
            part = mm(early, gram_ref[...]) + mm(later, late_early)
            result = result + mm(jnp.where(inside, part, 0.0), fold_ref[:width])
            part = mm_nt(early, late_early) + mm(later, late_late)
            result = result + mm(jnp.where(inside, part, 0.0), fold_ref[width:])
        left_ref[...] = result
    drain()


def eliminate(m, rank):
    row = lax.broadcasted_iota(jnp.int32, m.shape, 0)
    lane = lanes_of(m.shape)
    for k in range(0, rank, 2):
        line, after = m[k : k + 1, :], m[k + 1 : k + 2, :]
        column = jnp.broadcast_to(m[:, k : k + 1], m.shape)
        beside = jnp.broadcast_to(m[:, k + 1 : k + 2], m.shape)
        a, b, d = column[k : k + 1], column[k + 1 : k + 2], beside[k + 1 : k + 2]
        inverse = 1.0 / a
        ratio = b * inverse
        pivot = 1.0 / (d - ratio * b)
        after = after - ratio * line
        beside = (beside - ratio * column) * pivot
        m = (
            m
            - jnp.where(row > k, column * inverse, 0.0) * line
            - jnp.where(row > k + 1, beside, 0.0) * after
        )
    diagonal = jnp.sum(jnp.where(row == lane, m, 0.0), axis=1, keepdims=True)
    return m * lax.rsqrt(diagonal)


def in_two(x):
    high = x.astype(jnp.bfloat16)
    return high, (x - high.astype(jnp.float32)).astype(jnp.bfloat16)


CHUNK = 256


def merge_kernel(
    halves,
    left_ref,
    other_ref,
    spread_ref,
    unit_ref,
    expand_ref,
    kept_ref,
    came_ref,
    early_ref,
    late_ref,
    out_ref,
    end_ref,
    snap,
    out,
    arrived,
    left_sems,
    end_sems,
):
    me = lax.axis_index("tm")
    block = kept_ref.shape[2]
    ends = [
        pltpu.make_async_copy(
            ref, end_ref.at[:, :, pl.ds(pl.multiple_of(member * block, TILE), block)], end_sems.at[i]
        )
        for i, (ref, member) in enumerate(((kept_ref, me), (came_ref, 1 - me)))
    ]
    rank = left_ref.shape[0]
    wide = left_ref.shape[1]
    rows, width, length = snap.shape
    parts = length // CHUNK

    def fetch(i, part):
        at = pl.ds(i * CHUNK, CHUNK)
        ref = (early_ref, late_ref)[part]
        columns = pl.ds(part * (width // 2), width // 2)
        return pltpu.make_async_copy(ref.at[:, :, at], snap.at[:, columns, at], arrived.at[i, part])

    def store(i, half):
        at = pl.ds(half * length + i * CHUNK, CHUNK)
        return pltpu.make_async_copy(out.at[:, :, at], out_ref.at[:, :, at], left_sems.at[i, half])

    for i in range(parts):
        fetch(i, 0).start()
        fetch(i, 1).start()
    for copy in ends:
        copy.start()
    lane = lanes_of((rank, 128))
    whole = eliminate(mm(left_ref[...] + other_ref[...], spread_ref[...]) + unit_ref[...], rank)
    proj = jnp.where((lane >= rank) & (lane < rank + wide), whole, 0.0)
    outer = mm_nt(proj, proj)
    factor = eliminate(outer, rank)
    upper = jnp.where(
        lax.broadcasted_iota(jnp.int32, (rank, rank), 0) <= lanes_of((rank, rank)), factor, 0.0
    )
    mix = mm(upper, whole)
    weights = jnp.concatenate(
        [mm(mix, expand_ref[:, half * width : (half + 1) * width]) for half in range(halves)], axis=0
    )
    count = halves * rank
    high, low = in_two(weights)
    weights = jnp.concatenate(
        [jnp.concatenate([high, high], axis=1), jnp.concatenate([low, low], axis=1)], axis=0
    )
    for i in range(parts):
        fetch(i, 0).wait()
        fetch(i, 1).wait()
        for base in range(0, rows, 8):
            made = []
            for x in range(base, base + 8):
                values = jnp.concatenate(in_two(snap[x, :, i * CHUNK : (i + 1) * CHUNK]), axis=0)
                both = jnp.dot(weights, values, preferred_element_type=jnp.float32)
                made.append(both[:count] + both[count:])
            for half in range(halves):
                at = half * length + i * CHUNK
                for r in range(0, rank, 8):
                    first = half * rank + r
                    block = jnp.stack([p[first : first + 8] for p in made], axis=0)
                    out[r : r + 8, base : base + 8, at : at + CHUNK] = jnp.swapaxes(block, 0, 1)
        for half in range(halves):
            store(i, half).start()
    for i in range(parts):
        for half in range(halves):
            store(i, half).wait()
    for copy in ends:
        copy.wait()


def shifted(value, along_space, along_tm):
    space, tm = lax.axis_size("space"), lax.axis_size("tm")
    moves = [
        (s * tm + t, (s + along_space) % space * tm + (t + along_tm) % tm)
        for s in range(space)
        for t in range(tm)
    ]
    return lax.ppermute(value, AXES, moves)


def in_hbm(value):
    return pltpu.with_memory_space_constraint(value, pltpu.HBM)


def turn(value, start):
    return lax.dynamic_slice_in_dim(jnp.concatenate([value, value]), start, value.shape[0], 0)


def total_of(value):
    size = lax.axis_size("space") * lax.axis_size("tm")
    if size & (size - 1):
        return lax.psum(value, AXES), jnp.zeros_like(value)
    other = jnp.zeros_like(value)
    bit = 1
    while bit < size:
        value = value if bit == 1 else value + other
        other = lax.ppermute(value, AXES, [(i, i ^ bit) for i in range(size)])
        bit *= 2
    return value, other


def coefficients(gram, sketch):
    left = jnp.dot(sketch.T, gram, precision=HIGHEST)
    small = jnp.dot(left, sketch, precision=HIGHEST)
    lower = jnp.linalg.cholesky(small)
    proj = lax.linalg.triangular_solve(lower, left, left_side=True, lower=True)
    outer = jnp.dot(proj, proj.T, precision=HIGHEST)
    factor = jnp.linalg.cholesky(outer)
    mix = lax.linalg.triangular_solve(lower, factor, left_side=True, lower=True, transpose_a=True)
    return jnp.dot(sketch, mix, precision=HIGHEST)


def merge_levels(pieces, sketch):
    while pieces.shape[0] > 1:
        count, columns, rows, length = pieces.shape
        joined = pieces.reshape(count // 2, 2 * columns, rows, length)
        gram = jnp.einsum("gcxy,gdxy->gcd", joined, joined, precision=HIGHEST)
        gram = lax.psum(gram, AXES)
        coeff = jax.vmap(coefficients, in_axes=(0, None))(gram, sketch)
        pieces = jnp.einsum("gcxy,gcr->grxy", joined, coeff, precision=HIGHEST)
    return pieces[0]


def body(start_state, start_step, velocity_x, velocity_y, amplitude, frequency, phase, sketch):
    groups = lax.axis_size("tm")
    me = lax.axis_index("tm")
    rows, full = velocity_x.shape
    block = full // groups
    halves = max(1, 8 // (2 * groups))
    subs = halves * groups * 2
    length = block // halves
    span = length + TILE
    width = STEPS * subs
    fast = groups == 2
    f32 = jnp.float32

    total = rows + 2 * REACH
    shapes = [jax.ShapeDtypeStruct((7, count, block + TILE), f32) for count in (REACH, rows, REACH)]
    for _ in range(groups - 1):
        shapes += [jax.ShapeDtypeStruct((2, count, block + TILE), f32) for count in (REACH, rows, REACH)]
    packed = pl.pallas_call(
        functools.partial(pack_kernel, groups, block),
        out_shape=shapes,
        in_specs=[SMEM] + [HBM] * 6,
        out_specs=[VMEM] * len(shapes),
        scratch_shapes=[pltpu.VMEM(start_state.shape, f32)]
        + [pltpu.VMEM((rows, full), f32)] * 5
        + [pltpu.SemaphoreType.DMA((6,))],
        compiler_params=pltpu.CompilerParams(vmem_limit_bytes=16 * 2**20),
        name="pack",
    )(start_step, *map(in_hbm, (start_state, velocity_x, velocity_y, amplitude, frequency, phase)))
    sources = [shifted(packed[2], 1, 0), packed[1], shifted(packed[0], -1, 0)]
    for shift in range(1, groups):
        low, every, high = packed[3 * shift : 3 * shift + 3]
        sources += [shifted(high, 1, shift), shifted(every, 0, shift), shifted(low, -1, shift)]

    extra = []
    if fast:
        column = np.arange(width)
        half_of = column % subs // (2 * groups)
        picks = np.zeros((groups, halves, 2 * STEPS * groups, width), np.float32)
        for member in range(groups):
            group = (member - column % (2 * groups) // 2) % groups
            index = group * 2 * STEPS + column % 2 * STEPS + column // subs
            picks[member, half_of, index, column] = 1.0
        pick = lax.dynamic_index_in_dim(jnp.asarray(picks), me, 0, keepdims=False)
        pick = jnp.concatenate([pick[half] for half in range(halves)], axis=1)
        select = jnp.dot(sketch.T, pick, precision=HIGHEST)
        fold = sum(pick[:, half * width : (half + 1) * width] for half in range(halves)).T
        rank, wide = sketch.shape[1], sketch.shape[0]
        spread = jnp.concatenate(
            [sketch, jnp.eye(wide, dtype=f32), jnp.zeros((wide, 128 - rank - wide), f32)], axis=1
        )
        unit = jnp.eye(rank, 128, 128 - rank, dtype=f32)
        expand = jnp.concatenate([jnp.zeros((128 - rank, halves * width), f32), select], axis=0)
        extra = [select, fold]

    grid = [pltpu.VMEM((total + 2 * GUARD, subs, span), f32)] * 2 + [pltpu.VMEM((total, subs, span), f32)] * 2
    half_snap = (rows, width // 2, length)
    early, carry, low, own, high = pl.pallas_call(
        functools.partial(first_kernel, groups, halves),
        out_shape=[
            pltpu.HBM(half_snap, f32),
            jax.ShapeDtypeStruct((8, total, subs, span), f32),
            jax.ShapeDtypeStruct((REACH, subs, span), f32),
            jax.ShapeDtypeStruct((rows, subs, span), f32),
            jax.ShapeDtypeStruct((REACH, subs, span), f32),
        ],
        in_specs=[VMEM] * len(sources),
        out_specs=[HBM] + [VMEM] * 4,
        scratch_shapes=grid[:2] + [pltpu.VMEM(half_snap, f32), pltpu.SemaphoreType.DMA((REACH,))],
        compiler_params=pltpu.CompilerParams(vmem_limit_bytes=28 * 2**20),
        name="first",
    )(*sources)
    beside = [shifted(high, 1, 0), own, shifted(low, -1, 0)]
    outs = [
        pltpu.HBM(half_snap, f32),
        jax.ShapeDtypeStruct((2, rows, block), f32),
        jax.ShapeDtypeStruct((groups - 1, 2, rows, block), f32),
    ]
    if fast:
        outs.append(jax.ShapeDtypeStruct((sketch.shape[1], sketch.shape[0]), f32))
        gram = pl.pallas_call(
            gram_kernel,
            out_shape=jax.ShapeDtypeStruct((width // 2, width // 2), f32),
            in_specs=[HBM],
            out_specs=VMEM,
            scratch_shapes=[pltpu.VMEM(half_snap, f32), pltpu.SemaphoreType.DMA((4,))],
            cost_estimate=pl.CostEstimate(flops=2 * rows * width * width * length, bytes_accessed=2 * rows * width * length, transcendentals=0),
            compiler_params=pltpu.CompilerParams(vmem_limit_bytes=12 * 2**20),
            name="gram",
        )(in_hbm(early))
        extra = [gram] + extra
    made = pl.pallas_call(
        functools.partial(second_kernel, groups, halves, fast),
        out_shape=outs,
        in_specs=[VMEM] * (5 + len(extra)),
        out_specs=[HBM] + [VMEM] * (len(outs) - 1),
        scratch_shapes=grid[:4] + [pltpu.VMEM(half_snap, f32), pltpu.SemaphoreType.DMA((REACH,))],
        compiler_params=pltpu.CompilerParams(vmem_limit_bytes=32 * 2**20),
        name="second",
    )(*beside, carry, early, *extra)

    ends = [made[1]]
    for shift in range(1, groups):
        ends.append(shifted(made[2][shift - 1], 0, groups - shift))
    if fast:
        left, other = total_of(made[3])
        piece, end_state = pl.pallas_call(
            functools.partial(merge_kernel, halves),
            out_shape=[
                jax.ShapeDtypeStruct((rank, rows, block), f32),
                jax.ShapeDtypeStruct((2, rows, full), f32),
            ],
            in_specs=[VMEM] * 5 + [ANY] * 2 + [HBM] * 2,
            out_specs=[HBM] * 2,
            scratch_shapes=[
                pltpu.VMEM((rows, width, length), f32),
                pltpu.VMEM((rank, rows, block), f32),
                pltpu.SemaphoreType.DMA((length // CHUNK, 2)),
                pltpu.SemaphoreType.DMA((length // CHUNK, halves)),
                pltpu.SemaphoreType.DMA((2,)),
            ],
            compiler_params=pltpu.CompilerParams(vmem_limit_bytes=28 * 2**20),
            name="merge",
        )(left, other, spread, unit, expand, ends[0], ends[1], in_hbm(early), in_hbm(made[0]))
        return (piece, end_state[None])

    snaps = jnp.concatenate([early, made[0]], axis=1).reshape(rows, STEPS, halves, groups, 2, length)
    snaps = jnp.transpose(snaps, (3, 4, 1, 0, 2, 5)).reshape(groups, 2 * STEPS, rows, block)
    snaps = turn(jnp.flip(snaps, 0), groups - 1 - me)
    piece = merge_levels(snaps, sketch)
    stacked = turn(jnp.stack(ends), groups - me)
    end_state = jnp.moveaxis(stacked, 0, -2).reshape(2, rows, full)
    return (piece, end_state[None])


def solution(mesh):
    placed = (
        P("tm", None, "space", None),
        P("tm"),
        P("space", None),
        P("space", None),
        P("space", None),
        P("space", None),
        P("space", None),
        P(),
    )
    return jax.shard_map(
        body,
        mesh=mesh,
        in_specs=placed,
        out_specs=(P(None, "space", "tm"), P("tm", None, "space", None)),
        check_vma=False,
    )
```

```python
import functools

import jax
import jax.numpy as jnp
import numpy as np
from jax import lax
from jax.experimental import pallas as pl
from jax.experimental.pallas import tpu as pltpu
from jax.sharding import PartitionSpec as P

STEPS = 16
KAPPA = (0.06, 0.02)
HIGHEST = lax.Precision.HIGHEST
AXES = ("space", "tm")
TILE = 128
GUARD = 8
BATCH = 4
OWN = 8
REACH = STEPS // 2
VMEM = pl.BlockSpec(memory_space=pltpu.VMEM)
ANY = pl.BlockSpec(memory_space=pl.ANY)
HBM = pl.BlockSpec(memory_space=pltpu.HBM)
SMEM = pl.BlockSpec(memory_space=pltpu.SMEM)


def mm(a, b):
    return jnp.dot(a, b, precision=HIGHEST, preferred_element_type=jnp.float32)


def mm_nt(a, b):
    return lax.dot_general(
        a, b, (((1,), (1,)), ((), ())), precision=HIGHEST, preferred_element_type=jnp.float32
    )


def lanes_of(shape):
    return lax.broadcasted_iota(jnp.int32, shape, len(shape) - 1)


def pack_kernel(groups, block, step_ref, *refs):
    out_refs, scratch, sems = refs[6:-7], refs[-7:-1], refs[-1]
    brought = [pltpu.make_async_copy(refs[i], scratch[i], sems.at[i]) for i in range(6)]
    for copy in brought:
        copy.start()
    state_ref, vx, vy, amp, freq, phase = scratch
    full = vx.shape[1]
    me = lax.axis_index("tm")
    start = step_ref[0].astype(jnp.float32)
    rows = vx.shape[0]
    lane = lanes_of((rows, TILE))

    def cut(read, target, write, is_state):
        first = target * block
        write(pl.ds(0, block), read(pl.ds(pl.multiple_of(first, TILE), block)))
        above = jnp.minimum(first + block, full - TILE)
        below = jnp.maximum(first - TILE, 0)
        high = read(pl.ds(pl.multiple_of(above, TILE), TILE))
        low = read(pl.ds(pl.multiple_of(below, TILE), TILE))
        high = jnp.where(target < groups - 1, high, 0.0)
        low = jnp.where(target > 0, low, 0.0)
        halo = jnp.where(lane < TILE // 2, high, low)
        if is_state:
            halo = jnp.where((lane >= TILE // 4) & (lane < 3 * TILE // 4), start, halo)
        write(pl.ds(block, TILE), halo)

    def writer(group, index):
        low, every, high = out_refs[3 * group : 3 * group + 3]

        def write(columns, value):
            low[index, :, columns] = value[:REACH]
            every[index, :, columns] = value
            high[index, :, columns] = value[rows - REACH :]

        return write

    for index, ref in enumerate((vx, vy, amp, freq, phase)):
        brought[1 + index].wait()
        cut(lambda columns, ref=ref: ref[:, columns], me, writer(0, index), False)
    brought[0].wait()
    for shift in range(groups):
        target = lax.rem(me + shift, groups)
        for field in range(2):
            write = writer(shift, 5 + field if shift == 0 else field)
            cut(lambda columns, field=field: state_ref[0, field, :, columns], target, write, True)


def sin_cos(angle):
    turns = jnp.floor(angle * np.float32(2.0 / np.pi) + 0.5)
    r = angle - turns * np.float32(1.5703125)
    r = r - turns * np.float32(4.837512969970703125e-4)
    r = r - turns * np.float32(7.54978995489188216e-8)
    z = r * r
    sine = r + r * z * (
        np.float32(-1.6666654611e-1)
        + z * (np.float32(8.3321608736e-3) + z * np.float32(-1.9515295891e-4))
    )
    cosine = (
        1.0
        - 0.5 * z
        + z
        * z
        * (
            np.float32(4.166664568298827e-2)
            + z * (np.float32(-1.388731625493765e-3) + z * np.float32(2.443315711809948e-5))
        )
    )
    quadrant = turns.astype(jnp.int32)
    odd = (quadrant & 1) == 1
    s = jnp.where(odd, cosine, sine)
    c = jnp.where(odd, sine, cosine)
    s = jnp.where((quadrant & 2) == 2, -s, s)
    c = jnp.where(((quadrant + 1) & 2) == 2, -c, c)
    return s, c


def run_phase(grid, rows, snap, snap_ref, sems, keep_drift):
    qa, qb, xa, xb, twice, cw, ce, cs, cn, c0 = grid
    subs = qa.shape[1]
    tiles = qa.shape[2] // TILE
    total = rows + 2 * REACH

    for guard in (GUARD - 1, GUARD + total):
        qa[guard] = jnp.zeros(qa.shape[1:], jnp.float32)
        qb[guard] = jnp.zeros(qb.shape[1:], jnp.float32)

    lane2s = lanes_of((subs, TILE))
    first_lane, last_lane = lane2s == 0, lane2s == TILE - 1

    def advance(source, target, now, later, row, count, step, keep):
        def tile_of(r, t):
            return source[GUARD + row + r, :, t * TILE : (t + 1) * TILE]

        held, up, down = {}, {}, {}

        def load(t):
            for r in range(-1, count + 1):
                held[r, t] = tile_of(r, t)
            for r in range(count):
                up[r, t] = pltpu.roll(held[r, t], 1, 1)
                down[r, t] = pltpu.roll(held[r, t], TILE - 1, 1)

        load(tiles - 1)
        load(0)
        for r in range(count):
            up[r, -1], down[r, tiles] = up[r, tiles - 1], down[r, 0]
        for t in range(tiles):
            if t + 1 < tiles - 1:
                load(t + 1)
            cols = slice(t * TILE, (t + 1) * TILE)
            for r in range(count):
                x = row + r
                south = jnp.where(first_lane, up[r, t - 1], up[r, t])
                north = jnp.where(last_lane, down[r, t + 1], down[r, t])
                drive = now[x, :, cols]
                fresh = (
                    (c0[x, :, cols] * held[r, t] + cw[x, :, cols] * held[r - 1, t])
                    + (ce[x, :, cols] * held[r + 1, t] + cs[x, :, cols] * south)
                    + (cn[x, :, cols] * north + drive)
                )
                target[GUARD + x, :, cols] = fresh
                now[x, :, cols] = twice[x, :, cols] * later[x, :, cols] - drive
                if keep and t < tiles - 1:
                    snap[x - REACH, pl.ds(pl.multiple_of(step * subs, subs), subs), cols] = fresh

    def copy_out(step):
        part = pl.ds(pl.multiple_of(step * subs, subs), subs)
        return pltpu.make_async_copy(snap.at[:, part, :], snap_ref.at[:, part, :], sems.at[step])

    def one(source, target, now, later, step):
        low = (step + 1) // BATCH
        high = (total - 1 - step + BATCH - 1) // BATCH

        def halo_rows(i, carry):
            advance(source, target, now, later, i * BATCH, BATCH, step, False)
            return carry

        def own_rows(i, carry):
            advance(source, target, now, later, REACH + i * OWN, OWN, step, True)
            return carry

        def drift_rows(i, carry):
            part = pl.ds(i * BATCH, BATCH)
            now[part] = twice[part] * later[part] - now[part]
            return carry

        lax.fori_loop(0, rows // OWN, own_rows, 0)
        copy_out(step).start()
        lax.fori_loop(low, REACH // BATCH, halo_rows, 0)
        lax.fori_loop((REACH + rows) // BATCH, high, halo_rows, 0)
        if keep_drift:
            lax.fori_loop(0, low, drift_rows, 0)
            lax.fori_loop(high, total // BATCH, drift_rows, 0)

    def pair(i, carry):
        one(qa, qb, xa, xb, 2 * i)
        one(qb, qa, xb, xa, 2 * i + 1)
        return carry

    lax.fori_loop(0, REACH // 2, pair, 0)

    def drain():
        def drained(step, carry):
            copy_out(step).wait()
            return carry

        lax.fori_loop(0, REACH, drained, 0)

    return drain


def first_kernel(groups, halves, *refs):
    sources = [refs[3 * i : 3 * i + 3] for i in range(groups)]
    snap_ref, carry_ref, low_ref, own_ref, high_ref = refs[3 * groups : 3 * groups + 5]
    refs = refs[3 * groups + 5 :]
    qa, qb, snap, sems = refs
    xa, xb, twice, cw, ce, cs, cn, c0 = (carry_ref.at[i] for i in range(8))
    grid = (qa, qb, xa, xb, twice, cw, ce, cs, cn, c0)
    rows = sources[0][1].shape[1]
    block = sources[0][1].shape[2] - TILE
    length = block // halves
    tiles = length // TILE + 1
    subs = halves * groups * 2
    me = lax.axis_index("tm")
    offsets = (0, REACH, REACH + rows)

    sub = lax.broadcasted_iota(jnp.int32, (1, subs, TILE), 1)
    kappa = jnp.where((sub & 1) == 0, np.float32(KAPPA[0]), np.float32(KAPPA[1]))
    half_of = sub // (2 * groups)
    lane3 = lanes_of((1, subs, TILE))
    lowest = (me == 0) & (half_of == 0) & (lane3 >= TILE // 2)
    highest = (me == groups - 1) & (half_of == halves - 1) & (lane3 < TILE // 2)
    inside = jnp.where(lowest | highest, 0.0, 1.0).astype(jnp.float32)
    lane2 = lanes_of((8, TILE))

    def turned(parts):
        return jnp.swapaxes(jnp.stack(parts, axis=0), 0, 1)

    def prepare(place, base, tile, halo):
        def cut(ref, index, half):
            line = pl.ds(base, 8)
            if not halo:
                return ref[index, line, pl.ds(pl.multiple_of(half * length + tile * TILE, TILE), TILE)]
            above = (half + 1) * length
            below = half * length - TILE if half > 0 else block
            high = ref[index, line, above : above + TILE]
            if above == below:
                return high
            low = ref[index, line, below : below + TILE]
            return jnp.where(lane2 < TILE // 2, high, low)

        own = sources[0][place]
        starts, first, second, flow_x, flow_y, doubled = [], [], [], [], [], []
        for half in range(halves):
            vx, vy, amp, freq, phase = (cut(own, index, half) for index in range(5))
            sin_f, cos_f = sin_cos(freq)
            for group in range(groups):
                ref, at = sources[group][place], 5 if group == 0 else 0
                step = ref[at, pl.ds(base, 8), block : block + TILE][:, TILE // 2 : TILE // 2 + 1]
                s, c = sin_cos(freq * step + phase)
                s, c = amp * s, amp * c
                for field in range(2):
                    starts.append(cut(ref, at + field, half))
                    x, y = (s, c) if field == 0 else (0.5 * c, -0.5 * s)
                    first.append(x)
                    second.append(x * cos_f + y * sin_f)
                    flow_x.append(vx)
                    flow_y.append(vy)
                    doubled.append(2.0 * cos_f)
        where = pl.ds(offsets[place] + base, 8)
        columns = pl.ds(pl.multiple_of(tile * TILE, TILE), TILE)
        vx, vy = turned(flow_x), turned(flow_y)
        west = kappa + jnp.maximum(vx, 0.0)
        east = kappa - jnp.minimum(vx, 0.0)
        south = kappa + jnp.maximum(vy, 0.0)
        north = kappa - jnp.minimum(vy, 0.0)
        centre = 1.0 - (west + east + south + north)
        state, x0, x1 = turned(starts), turned(first), turned(second)
        if halo:
            west, east, south, north, centre, state, x0, x1 = (
                v * inside for v in (west, east, south, north, centre, state, x0, x1)
            )
        cw[where, :, columns] = west
        ce[where, :, columns] = east
        cs[where, :, columns] = south
        cn[where, :, columns] = north
        c0[where, :, columns] = centre
        xa[where, :, columns] = x0
        xb[where, :, columns] = x1
        twice[where, :, columns] = turned(doubled)
        qa[pl.ds(GUARD + offsets[place] + base, 8), :, columns] = state

    for place, count in ((0, REACH), (1, rows), (2, REACH)):

        def by_rows(number, carry, place=place):
            base = pl.multiple_of(number * 8, 8)

            def by_tiles(tile, inner):
                prepare(place, base, tile, False)
                return inner

            lax.fori_loop(0, tiles - 1, by_tiles, 0, unroll=4)
            prepare(place, base, tiles - 1, True)
            return carry

        lax.fori_loop(0, count // 8, by_rows, 0)

    drain = run_phase(grid, rows, snap, snap_ref, sems, True)
    low_ref[...] = qa[GUARD + REACH : GUARD + 2 * REACH]
    own_ref[...] = qa[GUARD + REACH : GUARD + REACH + rows]
    high_ref[...] = qa[GUARD + rows : GUARD + rows + REACH]
    drain()


def split_rows(a):
    high = a.astype(jnp.bfloat16)
    return jnp.concatenate([high, (a - high.astype(jnp.float32)).astype(jnp.bfloat16)], axis=0)


def outer_of(a, b):
    return lax.dot_general(a, b, (((1,), (1,)), ((), ())), preferred_element_type=jnp.float32)


def joined(g):
    m, n = g.shape[0] // 2, g.shape[1] // 2
    return (g[:m, :n] + g[m:, n:]) + (g[:m, n:] + g[m:, :n])


def gram_kernel(snap_ref, gram_ref, snap, sems):
    rows, width, _ = snap.shape
    parts = sems.shape[0]
    depth = rows // parts

    def fetch(i):
        at = pl.ds(i * depth, depth)
        return pltpu.make_async_copy(snap_ref.at[at], snap.at[at], sems.at[i])

    for i in range(parts):
        fetch(i).start()
    total = jnp.zeros((2 * width, 2 * width), jnp.float32)
    for i in range(parts):
        fetch(i).wait()
        for x in range(i * depth, (i + 1) * depth):
            both = split_rows(snap[x])
            total = total + outer_of(both, both)
    gram_ref[...] = joined(total)


def second_kernel(groups, halves, with_left, left_halo, own, right_halo, carry_ref, earlier, *refs):
    if with_left:
        gram_ref, select_ref, fold_ref = refs[:3]
        refs = refs[3:]
        snap_ref, kept_ref, sent_ref, left_ref = refs[:4]
        refs = refs[4:]
    else:
        snap_ref, kept_ref, sent_ref = refs[:3]
        refs = refs[3:]
    qa, qb, xa, xb, snap, sems = refs
    grid = [qa, qb, xa, xb] + [carry_ref.at[i] for i in range(2, 8)]
    rows, width, length = snap.shape
    subs = qa.shape[1]
    tiles = length // TILE + 1

    xa[...] = carry_ref[0]
    xb[...] = carry_ref[1]
    qa[GUARD : GUARD + REACH] = left_halo[...]
    qa[GUARD + REACH : GUARD + REACH + rows] = own[...]
    qa[GUARD + REACH + rows : GUARD + 2 * REACH + rows] = right_halo[...]
    drain = run_phase(grid, rows, snap, snap_ref, sems, False)

    for base in range(0, rows, 8):
        for t in range(tiles - 1):
            cols = slice(t * TILE, (t + 1) * TILE)
            value = jnp.swapaxes(qa[GUARD + REACH + base : GUARD + REACH + base + 8, :, cols], 0, 1)
            for half in range(halves):
                for group in range(groups):
                    for field in range(2):
                        end_ref = kept_ref if group == 0 else sent_ref.at[group - 1]
                        end_ref[field, base : base + 8, half * length + t * TILE : half * length + (t + 1) * TILE] = value[half * groups * 2 + group * 2 + field]

    if with_left:
        def add(x, total):
            now = split_rows(snap[x])
            every = jnp.concatenate([now, split_rows(earlier[x])], axis=0)
            return total + outer_of(now, every)

        both = jnp.zeros((2 * width, 4 * width), jnp.float32)
        for x in range(rows):
            both = add(x, both)
        late_late, late_early = joined(both[:, : 2 * width]), joined(both[:, 2 * width :])
        lane = lanes_of((1, width))
        result = jnp.zeros(left_ref.shape, jnp.float32)
        for half in range(halves):
            inside = (lane % subs) // (2 * groups) == half
            at = half * 2 * width
            early, later = select_ref[:, at : at + width], select_ref[:, at + width : at + 2 * width]
            part = mm(early, gram_ref[...]) + mm(later, late_early)
            result = result + mm(jnp.where(inside, part, 0.0), fold_ref[:width])
            part = mm_nt(early, late_early) + mm(later, late_late)
            result = result + mm(jnp.where(inside, part, 0.0), fold_ref[width:])
        left_ref[...] = result
    drain()


def eliminate(m, rank):
    row = lax.broadcasted_iota(jnp.int32, m.shape, 0)
    lane = lanes_of(m.shape)
    for k in range(0, rank, 2):
        line, after = m[k : k + 1, :], m[k + 1 : k + 2, :]
        column = jnp.broadcast_to(m[:, k : k + 1], m.shape)
        beside = jnp.broadcast_to(m[:, k + 1 : k + 2], m.shape)
        a, b, d = column[k : k + 1], column[k + 1 : k + 2], beside[k + 1 : k + 2]
        inverse = 1.0 / a
        ratio = b * inverse
        pivot = 1.0 / (d - ratio * b)
        after = after - ratio * line
        beside = (beside - ratio * column) * pivot
        m = (
            m
            - jnp.where(row > k, column * inverse, 0.0) * line
            - jnp.where(row > k + 1, beside, 0.0) * after
        )
    diagonal = jnp.sum(jnp.where(row == lane, m, 0.0), axis=1, keepdims=True)
    return m * lax.rsqrt(diagonal)


def in_two(x):
    high = x.astype(jnp.bfloat16)
    return high, (x - high.astype(jnp.float32)).astype(jnp.bfloat16)


CHUNK = 256


def merge_kernel(
    halves,
    left_ref,
    other_ref,
    spread_ref,
    unit_ref,
    expand_ref,
    kept_ref,
    came_ref,
    early_ref,
    late_ref,
    out_ref,
    end_ref,
    snap,
    out,
    arrived,
    left_sems,
    end_sems,
):
    me = lax.axis_index("tm")
    block = kept_ref.shape[2]
    ends = [
        pltpu.make_async_copy(
            ref, end_ref.at[:, :, pl.ds(pl.multiple_of(member * block, TILE), block)], end_sems.at[i]
        )
        for i, (ref, member) in enumerate(((kept_ref, me), (came_ref, 1 - me)))
    ]
    rank = left_ref.shape[0]
    wide = left_ref.shape[1]
    rows, width, length = snap.shape
    parts = length // CHUNK

    def fetch(i, part):
        at = pl.ds(i * CHUNK, CHUNK)
        ref = (early_ref, late_ref)[part]
        columns = pl.ds(part * (width // 2), width // 2)
        return pltpu.make_async_copy(ref.at[:, :, at], snap.at[:, columns, at], arrived.at[i, part])

    def store(i, half):
        at = pl.ds(half * length + i * CHUNK, CHUNK)
        return pltpu.make_async_copy(out.at[:, :, at], out_ref.at[:, :, at], left_sems.at[i, half])

    for i in range(parts):
        fetch(i, 0).start()
        fetch(i, 1).start()
    for copy in ends:
        copy.start()
    lane = lanes_of((rank, 128))
    whole = eliminate(mm(left_ref[...] + other_ref[...], spread_ref[...]) + unit_ref[...], rank)
    proj = jnp.where((lane >= rank) & (lane < rank + wide), whole, 0.0)
    outer = mm_nt(proj, proj)
    factor = eliminate(outer, rank)
    upper = jnp.where(
        lax.broadcasted_iota(jnp.int32, (rank, rank), 0) <= lanes_of((rank, rank)), factor, 0.0
    )
    mix = mm(upper, whole)
    weights = jnp.concatenate(
        [mm(mix, expand_ref[:, half * width : (half + 1) * width]) for half in range(halves)], axis=0
    )
    count = halves * rank
    high, low = in_two(weights)
    weights = jnp.concatenate(
        [jnp.concatenate([high, high], axis=1), jnp.concatenate([low, low], axis=1)], axis=0
    )
    for i in range(parts):
        fetch(i, 0).wait()
        fetch(i, 1).wait()
        for base in range(0, rows, 8):
            made = []
            for x in range(base, base + 8):
                values = jnp.concatenate(in_two(snap[x, :, i * CHUNK : (i + 1) * CHUNK]), axis=0)
                both = jnp.dot(weights, values, preferred_element_type=jnp.float32)
                made.append(both[:count] + both[count:])
            for half in range(halves):
                at = half * length + i * CHUNK
                for r in range(0, rank, 8):
                    first = half * rank + r
                    block = jnp.stack([p[first : first + 8] for p in made], axis=0)
                    out[r : r + 8, base : base + 8, at : at + CHUNK] = jnp.swapaxes(block, 0, 1)
        for half in range(halves):
            store(i, half).start()
    for i in range(parts):
        for half in range(halves):
            store(i, half).wait()
    for copy in ends:
        copy.wait()


def shifted(value, along_space, along_tm):
    space, tm = lax.axis_size("space"), lax.axis_size("tm")
    moves = [
        (s * tm + t, (s + along_space) % space * tm + (t + along_tm) % tm)
        for s in range(space)
        for t in range(tm)
    ]
    return lax.ppermute(value, AXES, moves)


def in_hbm(value):
    return pltpu.with_memory_space_constraint(value, pltpu.HBM)


def turn(value, start):
    return lax.dynamic_slice_in_dim(jnp.concatenate([value, value]), start, value.shape[0], 0)


def total_of(value):
    size = lax.axis_size("space") * lax.axis_size("tm")
    if size & (size - 1):
        return lax.psum(value, AXES), jnp.zeros_like(value)
    other = jnp.zeros_like(value)
    bit = 1
    while bit < size:
        value = value if bit == 1 else value + other
        other = lax.ppermute(value, AXES, [(i, i ^ bit) for i in range(size)])
        bit *= 2
    return value, other


def coefficients(gram, sketch):
    left = jnp.dot(sketch.T, gram, precision=HIGHEST)
    small = jnp.dot(left, sketch, precision=HIGHEST)
    lower = jnp.linalg.cholesky(small)
    proj = lax.linalg.triangular_solve(lower, left, left_side=True, lower=True)
    outer = jnp.dot(proj, proj.T, precision=HIGHEST)
    factor = jnp.linalg.cholesky(outer)
    mix = lax.linalg.triangular_solve(lower, factor, left_side=True, lower=True, transpose_a=True)
    return jnp.dot(sketch, mix, precision=HIGHEST)


def merge_levels(pieces, sketch):
    while pieces.shape[0] > 1:
        count, columns, rows, length = pieces.shape
        joined = pieces.reshape(count // 2, 2 * columns, rows, length)
        gram = jnp.einsum("gcxy,gdxy->gcd", joined, joined, precision=HIGHEST)
        gram = lax.psum(gram, AXES)
        coeff = jax.vmap(coefficients, in_axes=(0, None))(gram, sketch)
        pieces = jnp.einsum("gcxy,gcr->grxy", joined, coeff, precision=HIGHEST)
    return pieces[0]


def body(start_state, start_step, velocity_x, velocity_y, amplitude, frequency, phase, sketch):
    groups = lax.axis_size("tm")
    me = lax.axis_index("tm")
    rows, full = velocity_x.shape
    block = full // groups
    halves = max(1, 8 // (2 * groups))
    subs = halves * groups * 2
    length = block // halves
    span = length + TILE
    width = STEPS * subs
    fast = groups == 2
    f32 = jnp.float32

    total = rows + 2 * REACH
    shapes = [jax.ShapeDtypeStruct((7, count, block + TILE), f32) for count in (REACH, rows, REACH)]
    for _ in range(groups - 1):
        shapes += [jax.ShapeDtypeStruct((2, count, block + TILE), f32) for count in (REACH, rows, REACH)]
    packed = pl.pallas_call(
        functools.partial(pack_kernel, groups, block),
        out_shape=shapes,
        in_specs=[SMEM] + [HBM] * 6,
        out_specs=[VMEM] * len(shapes),
        scratch_shapes=[pltpu.VMEM(start_state.shape, f32)]
        + [pltpu.VMEM((rows, full), f32)] * 5
        + [pltpu.SemaphoreType.DMA((6,))],
        compiler_params=pltpu.CompilerParams(vmem_limit_bytes=16 * 2**20),
        name="pack",
    )(start_step, *map(in_hbm, (start_state, velocity_x, velocity_y, amplitude, frequency, phase)))
    sources = [shifted(packed[2], 1, 0), packed[1], shifted(packed[0], -1, 0)]
    for shift in range(1, groups):
        low, every, high = packed[3 * shift : 3 * shift + 3]
        sources += [shifted(high, 1, shift), shifted(every, 0, shift), shifted(low, -1, shift)]

    extra = []
    if fast:
        column = np.arange(width)
        half_of = column % subs // (2 * groups)
        picks = np.zeros((groups, halves, 2 * STEPS * groups, width), np.float32)
        for member in range(groups):
            group = (member - column % (2 * groups) // 2) % groups
            index = group * 2 * STEPS + column % 2 * STEPS + column // subs
            picks[member, half_of, index, column] = 1.0
        pick = lax.dynamic_index_in_dim(jnp.asarray(picks), me, 0, keepdims=False)
        pick = jnp.concatenate([pick[half] for half in range(halves)], axis=1)
        select = jnp.dot(sketch.T, pick, precision=HIGHEST)
        fold = sum(pick[:, half * width : (half + 1) * width] for half in range(halves)).T
        rank, wide = sketch.shape[1], sketch.shape[0]
        spread = jnp.concatenate(
            [sketch, jnp.eye(wide, dtype=f32), jnp.zeros((wide, 128 - rank - wide), f32)], axis=1
        )
        unit = jnp.eye(rank, 128, 128 - rank, dtype=f32)
        expand = jnp.concatenate([jnp.zeros((128 - rank, halves * width), f32), select], axis=0)
        extra = [select, fold]

    grid = [pltpu.VMEM((total + 2 * GUARD, subs, span), f32)] * 2 + [pltpu.VMEM((total, subs, span), f32)] * 2
    half_snap = (rows, width // 2, length)
    early, carry, low, own, high = pl.pallas_call(
        functools.partial(first_kernel, groups, halves),
        out_shape=[
            pltpu.HBM(half_snap, f32),
            jax.ShapeDtypeStruct((8, total, subs, span), f32),
            jax.ShapeDtypeStruct((REACH, subs, span), f32),
            jax.ShapeDtypeStruct((rows, subs, span), f32),
            jax.ShapeDtypeStruct((REACH, subs, span), f32),
        ],
        in_specs=[VMEM] * len(sources),
        out_specs=[HBM] + [VMEM] * 4,
        scratch_shapes=grid[:2] + [pltpu.VMEM(half_snap, f32), pltpu.SemaphoreType.DMA((REACH,))],
        compiler_params=pltpu.CompilerParams(vmem_limit_bytes=28 * 2**20),
        name="first",
    )(*sources)
    beside = [shifted(high, 1, 0), own, shifted(low, -1, 0)]
    outs = [
        pltpu.HBM(half_snap, f32),
        jax.ShapeDtypeStruct((2, rows, block), f32),
        jax.ShapeDtypeStruct((groups - 1, 2, rows, block), f32),
    ]
    if fast:
        outs.append(jax.ShapeDtypeStruct((sketch.shape[1], sketch.shape[0]), f32))
        gram = pl.pallas_call(
            gram_kernel,
            out_shape=jax.ShapeDtypeStruct((width // 2, width // 2), f32),
            in_specs=[HBM],
            out_specs=VMEM,
            scratch_shapes=[pltpu.VMEM(half_snap, f32), pltpu.SemaphoreType.DMA((4,))],
            cost_estimate=pl.CostEstimate(flops=2 * rows * width * width * length, bytes_accessed=2 * rows * width * length, transcendentals=0),
            compiler_params=pltpu.CompilerParams(vmem_limit_bytes=12 * 2**20),
            name="gram",
        )(in_hbm(early))
        extra = [gram] + extra
    made = pl.pallas_call(
        functools.partial(second_kernel, groups, halves, fast),
        out_shape=outs,
        in_specs=[VMEM] * (5 + len(extra)),
        out_specs=[HBM] + [VMEM] * (len(outs) - 1),
        scratch_shapes=grid[:4] + [pltpu.VMEM(half_snap, f32), pltpu.SemaphoreType.DMA((REACH,))],
        compiler_params=pltpu.CompilerParams(vmem_limit_bytes=32 * 2**20),
        name="second",
    )(*beside, carry, early, *extra)

    ends = [made[1]]
    for shift in range(1, groups):
        ends.append(shifted(made[2][shift - 1], 0, groups - shift))
    if fast:
        left, other = total_of(made[3])
        piece, end_state = pl.pallas_call(
            functools.partial(merge_kernel, halves),
            out_shape=[
                jax.ShapeDtypeStruct((rank, rows, block), f32),
                jax.ShapeDtypeStruct((2, rows, full), f32),
            ],
            in_specs=[VMEM] * 5 + [ANY] * 2 + [HBM] * 2,
            out_specs=[HBM] * 2,
            scratch_shapes=[
                pltpu.VMEM((rows, width, length), f32),
                pltpu.VMEM((rank, rows, block), f32),
                pltpu.SemaphoreType.DMA((length // CHUNK, 2)),
                pltpu.SemaphoreType.DMA((length // CHUNK, halves)),
                pltpu.SemaphoreType.DMA((2,)),
            ],
            compiler_params=pltpu.CompilerParams(vmem_limit_bytes=28 * 2**20),
            name="merge",
        )(left, other, spread, unit, expand, ends[0], ends[1], in_hbm(early), in_hbm(made[0]))
        return (piece, end_state[None])

    snaps = jnp.concatenate([early, made[0]], axis=1).reshape(rows, STEPS, halves, groups, 2, length)
    snaps = jnp.transpose(snaps, (3, 4, 1, 0, 2, 5)).reshape(groups, 2 * STEPS, rows, block)
    snaps = turn(jnp.flip(snaps, 0), groups - 1 - me)
    piece = merge_levels(snaps, sketch)
    stacked = turn(jnp.stack(ends), groups - me)
    end_state = jnp.moveaxis(stacked, 0, -2).reshape(2, rows, full)
    return (piece, end_state[None])


def solution(mesh):
    placed = (
        P("tm", None, "space", None),
        P("tm"),
        P("space", None),
        P("space", None),
        P("space", None),
        P("space", None),
        P("space", None),
        P(),
    )
    return jax.shard_map(
        body,
        mesh=mesh,
        in_specs=placed,
        out_specs=(P(None, "space", "tm"), P("tm", None, "space", None)),
        check_vma=False,
    )
```

```python
import functools

import jax
import jax.numpy as jnp
import numpy as np
from jax import lax
from jax.experimental import pallas as pl
from jax.experimental.pallas import tpu as pltpu
from jax.sharding import PartitionSpec as P

STEPS = 16
KAPPA = (0.06, 0.02)
HIGHEST = lax.Precision.HIGHEST
AXES = ("space", "tm")
TILE = 128
GUARD = 8
BATCH = 4
OWN = 8
REACH = STEPS // 2
VMEM = pl.BlockSpec(memory_space=pltpu.VMEM)
ANY = pl.BlockSpec(memory_space=pl.ANY)
HBM = pl.BlockSpec(memory_space=pltpu.HBM)
SMEM = pl.BlockSpec(memory_space=pltpu.SMEM)


def mm(a, b):
    return jnp.dot(a, b, precision=HIGHEST, preferred_element_type=jnp.float32)


def mm_nt(a, b):
    return lax.dot_general(
        a, b, (((1,), (1,)), ((), ())), precision=HIGHEST, preferred_element_type=jnp.float32
    )


def lanes_of(shape):
    return lax.broadcasted_iota(jnp.int32, shape, len(shape) - 1)


def pack_kernel(groups, block, step_ref, *refs):
    out_refs, scratch, sems = refs[6:-7], refs[-7:-1], refs[-1]
    brought = [pltpu.make_async_copy(refs[i], scratch[i], sems.at[i]) for i in range(6)]
    for copy in brought:
        copy.start()
    state_ref, vx, vy, amp, freq, phase = scratch
    full = vx.shape[1]
    me = lax.axis_index("tm")
    start = step_ref[0].astype(jnp.float32)
    rows = vx.shape[0]
    lane = lanes_of((rows, TILE))

    def cut(read, target, write, is_state):
        first = target * block
        write(pl.ds(0, block), read(pl.ds(pl.multiple_of(first, TILE), block)))
        above = jnp.minimum(first + block, full - TILE)
        below = jnp.maximum(first - TILE, 0)
        high = read(pl.ds(pl.multiple_of(above, TILE), TILE))
        low = read(pl.ds(pl.multiple_of(below, TILE), TILE))
        high = jnp.where(target < groups - 1, high, 0.0)
        low = jnp.where(target > 0, low, 0.0)
        halo = jnp.where(lane < TILE // 2, high, low)
        if is_state:
            halo = jnp.where((lane >= TILE // 4) & (lane < 3 * TILE // 4), start, halo)
        write(pl.ds(block, TILE), halo)

    def writer(group, index):
        low, every, high = out_refs[3 * group : 3 * group + 3]

        def write(columns, value):
            low[index, :, columns] = value[:REACH]
            every[index, :, columns] = value
            high[index, :, columns] = value[rows - REACH :]

        return write

    for index, ref in enumerate((vx, vy, amp, freq, phase)):
        brought[1 + index].wait()
        cut(lambda columns, ref=ref: ref[:, columns], me, writer(0, index), False)
    brought[0].wait()
    for shift in range(groups):
        target = lax.rem(me + shift, groups)
        for field in range(2):
            write = writer(shift, 5 + field if shift == 0 else field)
            cut(lambda columns, field=field: state_ref[0, field, :, columns], target, write, True)


def sin_cos(angle):
    turns = jnp.floor(angle * np.float32(2.0 / np.pi) + 0.5)
    r = angle - turns * np.float32(1.5703125)
    r = r - turns * np.float32(4.837512969970703125e-4)
    r = r - turns * np.float32(7.54978995489188216e-8)
    z = r * r
    sine = r + r * z * (
        np.float32(-1.6666654611e-1)
        + z * (np.float32(8.3321608736e-3) + z * np.float32(-1.9515295891e-4))
    )
    cosine = (
        1.0
        - 0.5 * z
        + z
        * z
        * (
            np.float32(4.166664568298827e-2)
            + z * (np.float32(-1.388731625493765e-3) + z * np.float32(2.443315711809948e-5))
        )
    )
    quadrant = turns.astype(jnp.int32)
    odd = (quadrant & 1) == 1
    s = jnp.where(odd, cosine, sine)
    c = jnp.where(odd, sine, cosine)
    s = jnp.where((quadrant & 2) == 2, -s, s)
    c = jnp.where(((quadrant + 1) & 2) == 2, -c, c)
    return s, c


def run_phase(grid, rows, snap, snap_ref, sems, keep_drift):
    qa, qb, xa, xb, twice, cw, ce, cs, cn, c0 = grid
    subs = qa.shape[1]
    tiles = qa.shape[2] // TILE
    total = rows + 2 * REACH

    for guard in (GUARD - 1, GUARD + total):
        qa[guard] = jnp.zeros(qa.shape[1:], jnp.float32)
        qb[guard] = jnp.zeros(qb.shape[1:], jnp.float32)

    lane2s = lanes_of((subs, TILE))
    first_lane, last_lane = lane2s == 0, lane2s == TILE - 1

    def advance(source, target, now, later, row, count, step, keep):
        def tile_of(r, t):
            return source[GUARD + row + r, :, t * TILE : (t + 1) * TILE]

        held, up, down = {}, {}, {}

        def load(t):
            for r in range(-1, count + 1):
                held[r, t] = tile_of(r, t)
            for r in range(count):
                up[r, t] = pltpu.roll(held[r, t], 1, 1)
                down[r, t] = pltpu.roll(held[r, t], TILE - 1, 1)

        load(tiles - 1)
        load(0)
        for r in range(count):
            up[r, -1], down[r, tiles] = up[r, tiles - 1], down[r, 0]
        for t in range(tiles):
            if t + 1 < tiles - 1:
                load(t + 1)
            cols = slice(t * TILE, (t + 1) * TILE)
            for r in range(count):
                x = row + r
                south = jnp.where(first_lane, up[r, t - 1], up[r, t])
                north = jnp.where(last_lane, down[r, t + 1], down[r, t])
                drive = now[x, :, cols]
                fresh = (
                    (c0[x, :, cols] * held[r, t] + cw[x, :, cols] * held[r - 1, t])
                    + (ce[x, :, cols] * held[r + 1, t] + cs[x, :, cols] * south)
                    + (cn[x, :, cols] * north + drive)
                )
                target[GUARD + x, :, cols] = fresh
                now[x, :, cols] = twice[x, :, cols] * later[x, :, cols] - drive
                if keep and t < tiles - 1:
                    snap[x - REACH, pl.ds(pl.multiple_of(step * subs, subs), subs), cols] = fresh

    def copy_out(step):
        part = pl.ds(pl.multiple_of(step * subs, subs), subs)
        return pltpu.make_async_copy(snap.at[:, part, :], snap_ref.at[:, part, :], sems.at[step])

    def one(source, target, now, later, step):
        low = (step + 1) // BATCH
        high = (total - 1 - step + BATCH - 1) // BATCH

        def halo_rows(i, carry):
            advance(source, target, now, later, i * BATCH, BATCH, step, False)
            return carry

        def own_rows(i, carry):
            advance(source, target, now, later, REACH + i * OWN, OWN, step, True)
            return carry

        def drift_rows(i, carry):
            part = pl.ds(i * BATCH, BATCH)
            now[part] = twice[part] * later[part] - now[part]
            return carry

        lax.fori_loop(0, rows // OWN, own_rows, 0)
        copy_out(step).start()
        lax.fori_loop(low, REACH // BATCH, halo_rows, 0)
        lax.fori_loop((REACH + rows) // BATCH, high, halo_rows, 0)
        if keep_drift:
            lax.fori_loop(0, low, drift_rows, 0)
            lax.fori_loop(high, total // BATCH, drift_rows, 0)

    def pair(i, carry):
        one(qa, qb, xa, xb, 2 * i)
        one(qb, qa, xb, xa, 2 * i + 1)
        return carry

    lax.fori_loop(0, REACH // 2, pair, 0)

    def drain():
        def drained(step, carry):
            copy_out(step).wait()
            return carry

        lax.fori_loop(0, REACH, drained, 0)

    return drain


def first_kernel(groups, halves, *refs):
    sources = [refs[3 * i : 3 * i + 3] for i in range(groups)]
    snap_ref, carry_ref, low_ref, own_ref, high_ref = refs[3 * groups : 3 * groups + 5]
    refs = refs[3 * groups + 5 :]
    qa, qb, snap, sems = refs
    xa, xb, twice, cw, ce, cs, cn, c0 = (carry_ref.at[i] for i in range(8))
    grid = (qa, qb, xa, xb, twice, cw, ce, cs, cn, c0)
    rows = sources[0][1].shape[1]
    block = sources[0][1].shape[2] - TILE
    length = block // halves
    tiles = length // TILE + 1
    subs = halves * groups * 2
    me = lax.axis_index("tm")
    offsets = (0, REACH, REACH + rows)

    sub = lax.broadcasted_iota(jnp.int32, (1, subs, TILE), 1)
    kappa = jnp.where((sub & 1) == 0, np.float32(KAPPA[0]), np.float32(KAPPA[1]))
    half_of = sub // (2 * groups)
    lane3 = lanes_of((1, subs, TILE))
    lowest = (me == 0) & (half_of == 0) & (lane3 >= TILE // 2)
    highest = (me == groups - 1) & (half_of == halves - 1) & (lane3 < TILE // 2)
    inside = jnp.where(lowest | highest, 0.0, 1.0).astype(jnp.float32)
    lane2 = lanes_of((8, TILE))

    def turned(parts):
        return jnp.swapaxes(jnp.stack(parts, axis=0), 0, 1)

    def prepare(place, base, tile, halo):
        def cut(ref, index, half):
            line = pl.ds(base, 8)
            if not halo:
                return ref[index, line, pl.ds(pl.multiple_of(half * length + tile * TILE, TILE), TILE)]
            above = (half + 1) * length
            below = half * length - TILE if half > 0 else block
            high = ref[index, line, above : above + TILE]
            if above == below:
                return high
            low = ref[index, line, below : below + TILE]
            return jnp.where(lane2 < TILE // 2, high, low)

        own = sources[0][place]
        starts, first, second, flow_x, flow_y, doubled = [], [], [], [], [], []
        for half in range(halves):
            vx, vy, amp, freq, phase = (cut(own, index, half) for index in range(5))
            sin_f, cos_f = sin_cos(freq)
            for group in range(groups):
                ref, at = sources[group][place], 5 if group == 0 else 0
                step = ref[at, pl.ds(base, 8), block : block + TILE][:, TILE // 2 : TILE // 2 + 1]
                s, c = sin_cos(freq * step + phase)
                s, c = amp * s, amp * c
                for field in range(2):
                    starts.append(cut(ref, at + field, half))
                    x, y = (s, c) if field == 0 else (0.5 * c, -0.5 * s)
                    first.append(x)
                    second.append(x * cos_f + y * sin_f)
                    flow_x.append(vx)
                    flow_y.append(vy)
                    doubled.append(2.0 * cos_f)
        where = pl.ds(offsets[place] + base, 8)
        columns = pl.ds(pl.multiple_of(tile * TILE, TILE), TILE)
        vx, vy = turned(flow_x), turned(flow_y)
        west = kappa + jnp.maximum(vx, 0.0)
        east = kappa - jnp.minimum(vx, 0.0)
        south = kappa + jnp.maximum(vy, 0.0)
        north = kappa - jnp.minimum(vy, 0.0)
        centre = 1.0 - (west + east + south + north)
        state, x0, x1 = turned(starts), turned(first), turned(second)
        if halo:
            west, east, south, north, centre, state, x0, x1 = (
                v * inside for v in (west, east, south, north, centre, state, x0, x1)
            )
        cw[where, :, columns] = west
        ce[where, :, columns] = east
        cs[where, :, columns] = south
        cn[where, :, columns] = north
        c0[where, :, columns] = centre
        xa[where, :, columns] = x0
        xb[where, :, columns] = x1
        twice[where, :, columns] = turned(doubled)
        qa[pl.ds(GUARD + offsets[place] + base, 8), :, columns] = state

    for place, count in ((0, REACH), (1, rows), (2, REACH)):

        def by_rows(number, carry, place=place):
            base = pl.multiple_of(number * 8, 8)

            def by_tiles(tile, inner):
                prepare(place, base, tile, False)
                return inner

            lax.fori_loop(0, tiles - 1, by_tiles, 0, unroll=4)
            prepare(place, base, tiles - 1, True)
            return carry

        lax.fori_loop(0, count // 8, by_rows, 0)

    drain = run_phase(grid, rows, snap, snap_ref, sems, True)
    low_ref[...] = qa[GUARD + REACH : GUARD + 2 * REACH]
    own_ref[...] = qa[GUARD + REACH : GUARD + REACH + rows]
    high_ref[...] = qa[GUARD + rows : GUARD + rows + REACH]
    drain()


def split_rows(a):
    high = a.astype(jnp.bfloat16)
    return jnp.concatenate([high, (a - high.astype(jnp.float32)).astype(jnp.bfloat16)], axis=0)


def outer_of(a, b):
    return lax.dot_general(a, b, (((1,), (1,)), ((), ())), preferred_element_type=jnp.float32)


def joined(g):
    m, n = g.shape[0] // 2, g.shape[1] // 2
    return (g[:m, :n] + g[m:, n:]) + (g[:m, n:] + g[m:, :n])


def gram_kernel(snap_ref, gram_ref, split_ref, snap, sems):
    rows, width, _ = snap.shape
    parts = sems.shape[0]
    depth = rows // parts

    def fetch(i):
        at = pl.ds(i * depth, depth)
        return pltpu.make_async_copy(snap_ref.at[at], snap.at[at], sems.at[i])

    for i in range(parts):
        fetch(i).start()
    total = jnp.zeros((2 * width, 2 * width), jnp.float32)
    for i in range(parts):
        fetch(i).wait()
        for x in range(i * depth, (i + 1) * depth):
            both = split_rows(snap[x])
            split_ref[x] = both
            total = total + outer_of(both, both)
    gram_ref[...] = joined(total)


def second_kernel(groups, halves, with_left, left_halo, own, right_halo, carry_ref, earlier, *refs):
    if with_left:
        gram_ref, select_ref, fold_ref = refs[:3]
        refs = refs[3:]
        snap_ref, kept_ref, sent_ref, left_ref = refs[:4]
        refs = refs[4:]
    else:
        snap_ref, kept_ref, sent_ref = refs[:3]
        refs = refs[3:]
    qa, qb, xa, xb, snap, sems = refs
    grid = [qa, qb, xa, xb] + [carry_ref.at[i] for i in range(2, 8)]
    rows, width, length = snap.shape
    subs = qa.shape[1]
    tiles = length // TILE + 1

    xa[...] = carry_ref[0]
    xb[...] = carry_ref[1]
    qa[GUARD : GUARD + REACH] = left_halo[...]
    qa[GUARD + REACH : GUARD + REACH + rows] = own[...]
    qa[GUARD + REACH + rows : GUARD + 2 * REACH + rows] = right_halo[...]
    drain = run_phase(grid, rows, snap, snap_ref, sems, False)

    for base in range(0, rows, 8):
        for t in range(tiles - 1):
            cols = slice(t * TILE, (t + 1) * TILE)
            value = jnp.swapaxes(qa[GUARD + REACH + base : GUARD + REACH + base + 8, :, cols], 0, 1)
            for half in range(halves):
                for group in range(groups):
                    for field in range(2):
                        end_ref = kept_ref if group == 0 else sent_ref.at[group - 1]
                        end_ref[field, base : base + 8, half * length + t * TILE : half * length + (t + 1) * TILE] = value[half * groups * 2 + group * 2 + field]

    if with_left:
        def add(x, total):
            now = split_rows(snap[x])
            every = jnp.concatenate([now, earlier[x]], axis=0)
            return total + outer_of(now, every)

        both = jnp.zeros((2 * width, 4 * width), jnp.float32)
        for x in range(rows):
            both = add(x, both)
        late_late, late_early = joined(both[:, : 2 * width]), joined(both[:, 2 * width :])
        lane = lanes_of((1, width))
        result = jnp.zeros(left_ref.shape, jnp.float32)
        for half in range(halves):
            inside = (lane % subs) // (2 * groups) == half
            at = half * 2 * width
            early, later = select_ref[:, at : at + width], select_ref[:, at + width : at + 2 * width]
            part = mm(early, gram_ref[...]) + mm(later, late_early)
            result = result + mm(jnp.where(inside, part, 0.0), fold_ref[:width])
            part = mm_nt(early, late_early) + mm(later, late_late)
            result = result + mm(jnp.where(inside, part, 0.0), fold_ref[width:])
        left_ref[...] = result
    drain()


def eliminate(m, rank):
    row = lax.broadcasted_iota(jnp.int32, m.shape, 0)
    lane = lanes_of(m.shape)
    for k in range(0, rank, 2):
        line, after = m[k : k + 1, :], m[k + 1 : k + 2, :]
        column = jnp.broadcast_to(m[:, k : k + 1], m.shape)
        beside = jnp.broadcast_to(m[:, k + 1 : k + 2], m.shape)
        a, b, d = column[k : k + 1], column[k + 1 : k + 2], beside[k + 1 : k + 2]
        inverse = 1.0 / a
        ratio = b * inverse
        pivot = 1.0 / (d - ratio * b)
        after = after - ratio * line
        beside = (beside - ratio * column) * pivot
        m = (
            m
            - jnp.where(row > k, column * inverse, 0.0) * line
            - jnp.where(row > k + 1, beside, 0.0) * after
        )
    diagonal = jnp.sum(jnp.where(row == lane, m, 0.0), axis=1, keepdims=True)
    return m * lax.rsqrt(diagonal)


def in_two(x):
    high = x.astype(jnp.bfloat16)
    return high, (x - high.astype(jnp.float32)).astype(jnp.bfloat16)


CHUNK = 256


def merge_kernel(
    halves,
    left_ref,
    other_ref,
    spread_ref,
    unit_ref,
    expand_ref,
    kept_ref,
    came_ref,
    early_ref,
    late_ref,
    out_ref,
    end_ref,
    snap,
    out,
    arrived,
    left_sems,
    end_sems,
):
    me = lax.axis_index("tm")
    block = kept_ref.shape[2]
    ends = [
        pltpu.make_async_copy(
            ref, end_ref.at[:, :, pl.ds(pl.multiple_of(member * block, TILE), block)], end_sems.at[i]
        )
        for i, (ref, member) in enumerate(((kept_ref, me), (came_ref, 1 - me)))
    ]
    rank = left_ref.shape[0]
    wide = left_ref.shape[1]
    rows, width, length = snap.shape
    parts = length // CHUNK

    def fetch(i, part):
        at = pl.ds(i * CHUNK, CHUNK)
        ref = (early_ref, late_ref)[part]
        columns = pl.ds(part * (width // 2), width // 2)
        return pltpu.make_async_copy(ref.at[:, :, at], snap.at[:, columns, at], arrived.at[i, part])

    def store(i, half):
        at = pl.ds(half * length + i * CHUNK, CHUNK)
        return pltpu.make_async_copy(out.at[:, :, at], out_ref.at[:, :, at], left_sems.at[i, half])

    for i in range(parts):
        fetch(i, 0).start()
        fetch(i, 1).start()
    for copy in ends:
        copy.start()
    lane = lanes_of((rank, 128))
    whole = eliminate(mm(left_ref[...] + other_ref[...], spread_ref[...]) + unit_ref[...], rank)
    proj = jnp.where((lane >= rank) & (lane < rank + wide), whole, 0.0)
    outer = mm_nt(proj, proj)
    factor = eliminate(outer, rank)
    upper = jnp.where(
        lax.broadcasted_iota(jnp.int32, (rank, rank), 0) <= lanes_of((rank, rank)), factor, 0.0
    )
    mix = mm(upper, whole)
    weights = jnp.concatenate(
        [mm(mix, expand_ref[:, half * width : (half + 1) * width]) for half in range(halves)], axis=0
    )
    count = halves * rank
    high, low = in_two(weights)
    weights = jnp.concatenate(
        [jnp.concatenate([high, high], axis=1), jnp.concatenate([low, low], axis=1)], axis=0
    )
    for i in range(parts):
        fetch(i, 0).wait()
        fetch(i, 1).wait()
        for base in range(0, rows, 8):
            made = []
            for x in range(base, base + 8):
                values = jnp.concatenate(in_two(snap[x, :, i * CHUNK : (i + 1) * CHUNK]), axis=0)
                both = jnp.dot(weights, values, preferred_element_type=jnp.float32)
                made.append(both[:count] + both[count:])
            for half in range(halves):
                at = half * length + i * CHUNK
                for r in range(0, rank, 8):
                    first = half * rank + r
                    block = jnp.stack([p[first : first + 8] for p in made], axis=0)
                    out[r : r + 8, base : base + 8, at : at + CHUNK] = jnp.swapaxes(block, 0, 1)
        for half in range(halves):
            store(i, half).start()
    for i in range(parts):
        for half in range(halves):
            store(i, half).wait()
    for copy in ends:
        copy.wait()


def shifted(value, along_space, along_tm):
    space, tm = lax.axis_size("space"), lax.axis_size("tm")
    moves = [
        (s * tm + t, (s + along_space) % space * tm + (t + along_tm) % tm)
        for s in range(space)
        for t in range(tm)
    ]
    return lax.ppermute(value, AXES, moves)


def in_hbm(value):
    return pltpu.with_memory_space_constraint(value, pltpu.HBM)


def turn(value, start):
    return lax.dynamic_slice_in_dim(jnp.concatenate([value, value]), start, value.shape[0], 0)


def total_of(value):
    size = lax.axis_size("space") * lax.axis_size("tm")
    if size & (size - 1):
        return lax.psum(value, AXES), jnp.zeros_like(value)
    other = jnp.zeros_like(value)
    bit = 1
    while bit < size:
        value = value if bit == 1 else value + other
        other = lax.ppermute(value, AXES, [(i, i ^ bit) for i in range(size)])
        bit *= 2
    return value, other


def coefficients(gram, sketch):
    left = jnp.dot(sketch.T, gram, precision=HIGHEST)
    small = jnp.dot(left, sketch, precision=HIGHEST)
    lower = jnp.linalg.cholesky(small)
    proj = lax.linalg.triangular_solve(lower, left, left_side=True, lower=True)
    outer = jnp.dot(proj, proj.T, precision=HIGHEST)
    factor = jnp.linalg.cholesky(outer)
    mix = lax.linalg.triangular_solve(lower, factor, left_side=True, lower=True, transpose_a=True)
    return jnp.dot(sketch, mix, precision=HIGHEST)


def merge_levels(pieces, sketch):
    while pieces.shape[0] > 1:
        count, columns, rows, length = pieces.shape
        joined = pieces.reshape(count // 2, 2 * columns, rows, length)
        gram = jnp.einsum("gcxy,gdxy->gcd", joined, joined, precision=HIGHEST)
        gram = lax.psum(gram, AXES)
        coeff = jax.vmap(coefficients, in_axes=(0, None))(gram, sketch)
        pieces = jnp.einsum("gcxy,gcr->grxy", joined, coeff, precision=HIGHEST)
    return pieces[0]


def body(start_state, start_step, velocity_x, velocity_y, amplitude, frequency, phase, sketch):
    groups = lax.axis_size("tm")
    me = lax.axis_index("tm")
    rows, full = velocity_x.shape
    block = full // groups
    halves = max(1, 8 // (2 * groups))
    subs = halves * groups * 2
    length = block // halves
    span = length + TILE
    width = STEPS * subs
    fast = groups == 2
    f32 = jnp.float32

    total = rows + 2 * REACH
    shapes = [jax.ShapeDtypeStruct((7, count, block + TILE), f32) for count in (REACH, rows, REACH)]
    for _ in range(groups - 1):
        shapes += [jax.ShapeDtypeStruct((2, count, block + TILE), f32) for count in (REACH, rows, REACH)]
    packed = pl.pallas_call(
        functools.partial(pack_kernel, groups, block),
        out_shape=shapes,
        in_specs=[SMEM] + [HBM] * 6,
        out_specs=[VMEM] * len(shapes),
        scratch_shapes=[pltpu.VMEM(start_state.shape, f32)]
        + [pltpu.VMEM((rows, full), f32)] * 5
        + [pltpu.SemaphoreType.DMA((6,))],
        compiler_params=pltpu.CompilerParams(vmem_limit_bytes=16 * 2**20),
        name="pack",
    )(start_step, *map(in_hbm, (start_state, velocity_x, velocity_y, amplitude, frequency, phase)))
    sources = [shifted(packed[2], 1, 0), packed[1], shifted(packed[0], -1, 0)]
    for shift in range(1, groups):
        low, every, high = packed[3 * shift : 3 * shift + 3]
        sources += [shifted(high, 1, shift), shifted(every, 0, shift), shifted(low, -1, shift)]

    extra = []
    if fast:
        column = np.arange(width)
        half_of = column % subs // (2 * groups)
        picks = np.zeros((groups, halves, 2 * STEPS * groups, width), np.float32)
        for member in range(groups):
            group = (member - column % (2 * groups) // 2) % groups
            index = group * 2 * STEPS + column % 2 * STEPS + column // subs
            picks[member, half_of, index, column] = 1.0
        pick = lax.dynamic_index_in_dim(jnp.asarray(picks), me, 0, keepdims=False)
        pick = jnp.concatenate([pick[half] for half in range(halves)], axis=1)
        select = jnp.dot(sketch.T, pick, precision=HIGHEST)
        fold = sum(pick[:, half * width : (half + 1) * width] for half in range(halves)).T
        rank, wide = sketch.shape[1], sketch.shape[0]
        spread = jnp.concatenate(
            [sketch, jnp.eye(wide, dtype=f32), jnp.zeros((wide, 128 - rank - wide), f32)], axis=1
        )
        unit = jnp.eye(rank, 128, 128 - rank, dtype=f32)
        expand = jnp.concatenate([jnp.zeros((128 - rank, halves * width), f32), select], axis=0)
        extra = [select, fold]

    grid = [pltpu.VMEM((total + 2 * GUARD, subs, span), f32)] * 2 + [pltpu.VMEM((total, subs, span), f32)] * 2
    half_snap = (rows, width // 2, length)
    early, carry, low, own, high = pl.pallas_call(
        functools.partial(first_kernel, groups, halves),
        out_shape=[
            pltpu.HBM(half_snap, f32),
            jax.ShapeDtypeStruct((8, total, subs, span), f32),
            jax.ShapeDtypeStruct((REACH, subs, span), f32),
            jax.ShapeDtypeStruct((rows, subs, span), f32),
            jax.ShapeDtypeStruct((REACH, subs, span), f32),
        ],
        in_specs=[VMEM] * len(sources),
        out_specs=[HBM] + [VMEM] * 4,
        scratch_shapes=grid[:2] + [pltpu.VMEM(half_snap, f32), pltpu.SemaphoreType.DMA((REACH,))],
        compiler_params=pltpu.CompilerParams(vmem_limit_bytes=28 * 2**20),
        name="first",
    )(*sources)
    beside = [shifted(high, 1, 0), own, shifted(low, -1, 0)]
    outs = [
        pltpu.HBM(half_snap, f32),
        jax.ShapeDtypeStruct((2, rows, block), f32),
        jax.ShapeDtypeStruct((groups - 1, 2, rows, block), f32),
    ]
    if fast:
        outs.append(jax.ShapeDtypeStruct((sketch.shape[1], sketch.shape[0]), f32))
        gram, split = pl.pallas_call(
            gram_kernel,
            out_shape=[
                jax.ShapeDtypeStruct((width // 2, width // 2), f32),
                jax.ShapeDtypeStruct((rows, width, length), jnp.bfloat16),
            ],
            in_specs=[HBM],
            out_specs=[VMEM] * 2,
            scratch_shapes=[pltpu.VMEM(half_snap, f32), pltpu.SemaphoreType.DMA((4,))],
            cost_estimate=pl.CostEstimate(flops=2 * rows * width * width * length, bytes_accessed=2 * rows * width * length, transcendentals=0),
            compiler_params=pltpu.CompilerParams(vmem_limit_bytes=16 * 2**20),
            name="gram",
        )(in_hbm(early))
        extra = [gram] + extra
    else:
        split = early
    made = pl.pallas_call(
        functools.partial(second_kernel, groups, halves, fast),
        out_shape=outs,
        in_specs=[VMEM] * (5 + len(extra)),
        out_specs=[HBM] + [VMEM] * (len(outs) - 1),
        scratch_shapes=grid[:4] + [pltpu.VMEM(half_snap, f32), pltpu.SemaphoreType.DMA((REACH,))],
        compiler_params=pltpu.CompilerParams(vmem_limit_bytes=32 * 2**20),
        name="second",
    )(*beside, carry, split, *extra)

    ends = [made[1]]
    for shift in range(1, groups):
        ends.append(shifted(made[2][shift - 1], 0, groups - shift))
    if fast:
        left, other = total_of(made[3])
        piece, end_state = pl.pallas_call(
            functools.partial(merge_kernel, halves),
            out_shape=[
                jax.ShapeDtypeStruct((rank, rows, block), f32),
                jax.ShapeDtypeStruct((2, rows, full), f32),
            ],
            in_specs=[VMEM] * 5 + [ANY] * 2 + [HBM] * 2,
            out_specs=[HBM] * 2,
            scratch_shapes=[
                pltpu.VMEM((rows, width, length), f32),
                pltpu.VMEM((rank, rows, block), f32),
                pltpu.SemaphoreType.DMA((length // CHUNK, 2)),
                pltpu.SemaphoreType.DMA((length // CHUNK, halves)),
                pltpu.SemaphoreType.DMA((2,)),
            ],
            compiler_params=pltpu.CompilerParams(vmem_limit_bytes=28 * 2**20),
            name="merge",
        )(left, other, spread, unit, expand, ends[0], ends[1], in_hbm(early), in_hbm(made[0]))
        return (piece, end_state[None])

    snaps = jnp.concatenate([early, made[0]], axis=1).reshape(rows, STEPS, halves, groups, 2, length)
    snaps = jnp.transpose(snaps, (3, 4, 1, 0, 2, 5)).reshape(groups, 2 * STEPS, rows, block)
    snaps = turn(jnp.flip(snaps, 0), groups - 1 - me)
    piece = merge_levels(snaps, sketch)
    stacked = turn(jnp.stack(ends), groups - me)
    end_state = jnp.moveaxis(stacked, 0, -2).reshape(2, rows, full)
    return (piece, end_state[None])


def solution(mesh):
    placed = (
        P("tm", None, "space", None),
        P("tm"),
        P("space", None),
        P("space", None),
        P("space", None),
        P("space", None),
        P("space", None),
        P(),
    )
    return jax.shard_map(
        body,
        mesh=mesh,
        in_specs=placed,
        out_specs=(P(None, "space", "tm"), P("tm", None, "space", None)),
        check_vma=False,
    )
```
